128 devices in a mesh: section: 8 (over y_hi, x), dp: 16 (over y_lo, z, core).
Axes of the slice: x: 4, y: 4 (y_hi: 2, y_lo: 2; y = y_hi * 2 + y_lo), z: 4, core: 2. Of those that a mesh axis runs over, the one named last changes fastest.
Arguments:
- inputs: bfloat16 [2, 1024, 4096], P(None, 'dp'), may hold values from -6 to 6
- cotangent: bfloat16 [2, 1024, 4096], P(None, 'dp'), may hold values from -0.13183594 to 0.13183594
- w_in: bfloat16 [16, 4096, 256], P('section'), as said below
- w_out: bfloat16 [16, 256, 4096], P('section'), as said below
- gain: float32 [16, 4096], P('section'), as said below
Outputs:
- grad_in: float32 [8, 4096, 256], P('section', 'dp')
- grad_out: float32 [8, 256, 4096], P('section', None, 'dp')
- grad_gain: float32 [8, 4096], P('section', 'dp')
The draws below stay inside these ranges and needn't reach their ends.
Inputs may be any that keep to these rules, and one draw needn't show every extreme that they name: `w_in`: rows 2 j and 2 (7 - j) + 1 hold the same layer j, so that a device holds a layer of the down relay and the mirrored layer of the up relay. `w_out`: rows 2 j and 2 (7 - j) + 1 hold the same layer j. `gain`: rows 2 j and 2 (7 - j) + 1 hold the same layer j.
All inputs are finite; a program needn't handle non-finite values.
Results may differ from the reference program's by a relative error of at most 0.03.
Values may be sent and summed in bfloat16 or wider, within the bound.
No kernel may reach another device: no remote copies, remote signals or barrier semaphores. Data moves between devices by JAX's collectives and lax.ppermute only.
A program may use at most 128 MiB of HBM per device.

```python
import jax
import jax.numpy as jnp
from jax import lax

D = 4096
BRANCH = 256
ROWS = 64
TOKENS = 1024
LAYERS = 8
N_DP = 16


def mirrored(base):
    layer_ids = jnp.arange(LAYERS, dtype=jnp.int32)
    order = jnp.stack([layer_ids, LAYERS - 1 - layer_ids], axis=1).reshape(-1)
    return base[order]


def draw_w_in(key, part):
    key = jax.random.fold_in(key, 11)
    base = jax.random.normal(key, (LAYERS, D, BRANCH), jnp.float32) * D ** (-0.5)
    return mirrored(base).astype(jnp.bfloat16)


def draw_w_out(key, part):
    key = jax.random.fold_in(key, 23)
    base = jax.random.normal(key, (LAYERS, BRANCH, D), jnp.float32) * BRANCH ** (-0.5)
    return mirrored(base).astype(jnp.bfloat16)


def draw_gain(key, part):
    key = jax.random.fold_in(key, 37)
    base = jax.random.uniform(key, (LAYERS, D), jnp.float32, 0.5, 1.5)
    return mirrored(base)


def with_spikes(result, rng, source, target, blocks, factor):
    def block_of(dim):
        return (jnp.arange(result.shape[dim]) // (result.shape[dim] // blocks)).reshape((-1,) + (1,) * (result.ndim - 1 - dim))

    first = jax.random.permutation(rng, blocks)[block_of(target)]
    far = (block_of(target) + blocks // 2) % blocks
    return jnp.where((block_of(source) == first) | (block_of(source) == far), factor * result, result)


def block_levels(stream_key, extent, shards, smallest, high):
    level, own = 1.0, jax.random.fold_in(stream_key, 6)
    for position, parts in shards:
        heights = jnp.exp(jax.random.uniform(jax.random.fold_in(own, position), (parts,), jnp.float32, smallest / len(shards), high / len(shards)))
        level = level * jnp.repeat(heights, extent[position] // parts).reshape([-1 if axis == position else 1 for axis in range(len(extent))])
    return level


def bell_draw(rng, dims, scale, most, shards=(), kind=jnp.bfloat16):
    array = scale * jax.random.normal(rng, dims, jnp.float32)
    if shards:
        array = array * block_levels(rng, dims, shards, -0.22, 0.18)
    return jnp.clip(array, -most, most).astype(kind)


def bell_draw_with(key, dims, width, limit, pieces, heavy, kind=jnp.bfloat16):
    entries = width * jax.random.normal(key, dims, jnp.float32)
    if pieces:
        entries = entries * block_levels(key, dims, pieces, -0.22, 0.18)
    return jnp.clip(with_spikes(entries, jax.random.fold_in(key, 3), *heavy), -limit, limit).astype(kind)


def setup_inputs(seed: int = 0) -> dict:
    key_of = jax.random.split(jax.random.key(seed), 6)
    return {
        "inputs": bell_draw(key_of[0], (2, TOKENS, D), 1.0, 6.0, ((1, 16),)),
        "cotangent": bell_draw_with(key_of[1], (2, TOKENS, D), (1.0 / (2 * TOKENS) ** 0.5), 0.13183594, ((1, 16),), (1, 2, 16, 2.0)),
        "w_in": draw_w_in(jax.random.fold_in(key_of[5], 71), 0),
        "w_out": draw_w_out(jax.random.fold_in(key_of[5], 71), 0),
        "gain": draw_gain(jax.random.fold_in(key_of[5], 71), 0),
    }


epsilon = 1e-05

def right_product(left, weight):
    return lax.dot_general(left, weight, (((1,), (1,)), ((), ())), preferred_element_type=jnp.float32)

def norm_parts(source, gain_row, weight_in):
    wide = source.astype(jnp.float32)
    scaling = lax.rsqrt(lax.optimization_barrier(jnp.mean(wide * wide, axis=-1, keepdims=True)) + epsilon)
    normed = (wide * scaling * gain_row).astype(jnp.bfloat16)
    before = jnp.dot(normed, weight_in, preferred_element_type=jnp.float32)
    return (wide, scaling, normed, before)

def layer_output(source, gain_row, weight_in, weight_out):
    wide, scaling, normed, before = norm_parts(source, gain_row, weight_in)
    inner = (before * jax.nn.sigmoid(before)).astype(jnp.bfloat16)
    return (wide + jnp.dot(inner, weight_out, preferred_element_type=jnp.float32)).astype(jnp.bfloat16)

def layer_backward(source, upstream, gain_row, weight_in, weight_out, before):
    wide = source.astype(jnp.float32)
    scaling = lax.rsqrt(lax.optimization_barrier(jnp.mean(wide * wide, axis=-1, keepdims=True)) + epsilon)
    sigma = jax.nn.sigmoid(before)
    inner = (before * sigma).astype(jnp.bfloat16)
    d_inner = right_product(upstream, weight_out)
    d_before = (d_inner * sigma * (1.0 + before * (1.0 - sigma))).astype(jnp.bfloat16)
    d_normed = right_product(d_before, weight_in)
    gain_rows = d_normed * wide * scaling
    scaled = d_normed * gain_row
    mixed = lax.optimization_barrier(jnp.mean(scaled * wide, axis=-1, keepdims=True))
    d_source = (upstream.astype(jnp.float32) + scaling * (scaled - wide * scaling * scaling * mixed)).astype(jnp.bfloat16)
    return (d_source, inner, d_before, gain_rows)

def rounded_sum(terms):
    rounded = lax.optimization_barrier(terms.astype(jnp.bfloat16))
    return lax.optimization_barrier(jnp.sum(rounded.astype(jnp.float32), axis=0))

def partial_sum(left, right):
    terms = jnp.einsum('grd,grh->gdh', left.astype(jnp.float32), right.astype(jnp.float32))
    return rounded_sum(terms)

def reference(inputs, cotangent, w_in, w_out, gain):
    groups = 2 * N_DP
    state = inputs.reshape(2 * TOKENS, D)
    saved = []
    for layer in range(LAYERS):
        saved.append(state)
        state = layer_output(state, gain[2 * layer], w_in[2 * layer], w_out[2 * layer])
    upstream = cotangent.reshape(2 * TOKENS, D)
    grads_in = [None] * LAYERS
    grads_out = [None] * LAYERS
    grads_gain = [None] * LAYERS
    for layer in reversed(range(LAYERS)):
        source = saved[layer]
        wide, scaling, normed, before = norm_parts(source, gain[2 * layer], w_in[2 * layer])
        d_source, inner, d_before, gain_rows = layer_backward(source, upstream, gain[2 * layer], w_in[2 * layer], w_out[2 * layer], before)
        grads_in[layer] = partial_sum(normed.reshape(groups, ROWS, D), d_before.reshape(groups, ROWS, BRANCH))
        grads_out[layer] = partial_sum(inner.reshape(groups, ROWS, BRANCH), upstream.reshape(groups, ROWS, D))
        grads_gain[layer] = rounded_sum(lax.optimization_barrier(jnp.sum(gain_rows.reshape(groups, ROWS, D), axis=1)))
        upstream = d_source
    return (jnp.stack(grads_in), jnp.stack(grads_out), jnp.stack(grads_gain))
```

```python
import functools

import jax
import jax.numpy as jnp
from jax import lax
from jax.experimental import pallas as pl
from jax.experimental.pallas import tpu as pltpu
from jax.sharding import PartitionSpec as P

epsilon = 1e-05
STAGES = (0, 1, 2, 3, 2, 1, 0, 1, 2, 3, 2, 1, 0)
LAST = len(STAGES) - 1
MICROS = 2
bf16 = jnp.bfloat16
f32 = jnp.float32


def matmul(left, right):
    return jnp.dot(left, right, preferred_element_type=f32)


def transpose_weights(weight_in, weight_out, weight_in_t, weight_out_t):
    width, branch = weight_in.shape[1:]
    for copy in range(2):

        @pl.loop(0, width // branch)
        def _(tile):
            part = pl.ds(pl.multiple_of(tile * branch, branch), branch)
            weight_in_t[copy, :, part] = weight_in[copy, part, :].T
            weight_out_t[copy, part, :] = weight_out[copy, :, part].T


def stage_kernel(step, place_ref, *refs):
    (moved, inputs, cotangent, weight_in, weight_out, gain), refs = refs[:6], refs[6:]
    if step:
        refs = refs[8:]
    sent, weight_in_t, weight_out_t, hat, upstream, pre_all, scale_all, inner_all, delta_all = refs
    place, half = place_ref[0], place_ref[1]
    first, second = half, 1 - half
    micro = moved.shape[0]
    width = moved.shape[1]

    def forward(source, copy, rows, last=False):
        wide = source.astype(f32)
        scaling = lax.rsqrt(jnp.mean(wide * wide, axis=-1, keepdims=True) + epsilon)
        normal = wide * scaling
        hat[copy, rows, :] = normal.astype(bf16)
        before = matmul((normal * gain[copy]).astype(bf16), weight_in[copy])
        inner = (before * jax.nn.sigmoid(before)).astype(bf16)
        pre_all[copy, rows, :] = before
        scale_all[copy, rows, :] = jnp.broadcast_to(scaling, (micro, 128))
        inner_all[copy, rows, :] = inner
        if not last:
            return (wide + matmul(inner, weight_out[copy])).astype(bf16)

    def backward(grad, copy, rows, last=False):
        upstream[copy, rows, :] = grad
        before = pre_all[copy, rows, :]
        sigma = jax.nn.sigmoid(before)
        d_inner = matmul(grad, weight_out_t[copy])
        delta = (d_inner * sigma * (1.0 + before * (1.0 - sigma))).astype(bf16)
        delta_all[copy, rows, :] = delta
        if not last:
            mixed = jnp.sum(delta.astype(f32) * before, axis=-1, keepdims=True) / width
            scaled = matmul(delta, weight_in_t[copy]) * gain[copy]
            scaling = scale_all[copy, rows, :1]
            normal = hat[copy, rows, :].astype(f32)
            return (grad.astype(f32) + scaling * (scaled - normal * mixed)).astype(bf16)

    def run(stage, micro_batch):
        rows = pl.ds(micro_batch * micro, micro)
        if stage == 0:
            sent[...] = forward(inputs[half, rows, :], first, rows)
        elif stage < 3:
            sent[...] = forward(moved[...], first, rows)
        elif stage == 3:
            sent[...] = forward(moved[...], first, rows)
            sent[...] = forward(sent[...], second, rows)
        elif stage < 6:
            sent[...] = forward(moved[...], second, rows)
        elif stage == 6:
            forward(moved[...], second, rows, last=True)
            sent[...] = backward(cotangent[half, rows, :], second, rows)
        elif stage < 9:
            sent[...] = backward(moved[...], second, rows)
        elif stage == 9:
            sent[...] = backward(moved[...], second, rows)
            sent[...] = backward(sent[...], first, rows)
        elif stage < LAST:
            sent[...] = backward(moved[...], first, rows)
        else:
            backward(moved[...], first, rows, last=True)

    for micro_batch in range(MICROS):
        stage = step - micro_batch
        if 0 <= stage <= LAST:
            pl.when(place == STAGES[stage])(functools.partial(run, stage, micro_batch))

    idle = {0: (2, 3), 3: (0, 1)}.get(step)
    if idle:

        @pl.when((place == idle[0]) | (place == idle[1]))
        def _():
            transpose_weights(weight_in, weight_out, weight_in_t, weight_out_t)


def run_stage(step, place, moved, fixed, state):
    micro, width = moved.shape
    rows = micro * MICROS
    branch = fixed[2].shape[2]
    vmem = pl.BlockSpec(memory_space=pltpu.VMEM)
    outs = (
        pltpu.VMEM((micro, width), bf16),
        pltpu.VMEM((2, branch, width), bf16),
        pltpu.VMEM((2, width, branch), bf16),
        pltpu.VMEM((2, rows, width), bf16),
        pltpu.VMEM((2, rows, width), bf16),
        pltpu.VMEM((2, rows, branch), f32),
        pltpu.VMEM((2, rows, 128), f32),
        pltpu.VMEM((2, rows, branch), bf16),
        pltpu.VMEM((2, rows, branch), bf16),
    )
    aliases = {7 + i: 1 + i for i in range(len(state))}
    result = pl.pallas_call(
        functools.partial(stage_kernel, step),
        out_shape=outs,
        in_specs=[pl.BlockSpec(memory_space=pltpu.SMEM)] + [vmem] * (6 + len(state)),
        out_specs=(vmem,) * len(outs),
        input_output_aliases=aliases,
        compiler_params=pltpu.CompilerParams(vmem_limit_bytes=16 * 2**20),
        cost_estimate=pl.CostEstimate(flops=10**9, bytes_accessed=4 * 2**20, transcendentals=0),
        name="stage_%d" % step,
    )(place, moved, *fixed, *state)
    return result[0], result[1:]


def load_kernel(source_in, source_out, weight_in, weight_out, sems):
    copies = [
        pltpu.make_async_copy(source_in, weight_in, sems.at[0]),
        pltpu.make_async_copy(source_out, weight_out, sems.at[1]),
    ]
    for copy in copies:
        copy.start()
    for copy in copies:
        copy.wait()


def on_device(inputs, cotangent, w_in, w_out, gain):
    sections = lax.axis_size("section")
    parts = lax.axis_size("dp")
    position = lax.axis_index("section")
    half = (position >= sections // 2).astype(jnp.int32)
    fold = jnp.where(half == 0, position, sections - 1 - position).astype(jnp.int32)
    place = jnp.stack([fold, half])
    rows, width = inputs.shape[1:]
    micro = rows // MICROS
    branch = w_in.shape[2]

    vmem = pl.BlockSpec(memory_space=pltpu.VMEM)
    weights = pl.pallas_call(
        load_kernel,
        out_shape=(pltpu.VMEM(w_in.shape, bf16), pltpu.VMEM(w_out.shape, bf16)),
        in_specs=[pl.BlockSpec(memory_space=pl.ANY)] * 2,
        out_specs=(vmem, vmem),
        scratch_shapes=[pltpu.SemaphoreType.DMA((2,))],
        compiler_params=pltpu.CompilerParams(vmem_limit_bytes=16 * 2**20),
        name="load",
    )(w_in, w_out)
    fixed = (inputs, cotangent, *weights, gain[:, None, :])

    def both_halves(pairs):
        return pairs + [(sections - 1 - a, sections - 1 - b) for a, b in pairs]

    moved = inputs[0, :micro]
    state = ()
    for step in range(LAST + MICROS):
        sent, state = run_stage(step, place, moved, fixed, state)
        pairs = [
            (STAGES[step - m], STAGES[step - m + 1])
            for m in range(MICROS)
            if 0 <= step - m < LAST
        ]
        if pairs:
            moved = lax.ppermute(sent, "section", both_halves(pairs))

    _, _, hat, upstream, _, _, inner, delta = state
    narrow = jnp.concatenate([delta, inner])
    payload = jnp.concatenate([hat, upstream, jnp.tile(narrow, (1, 1, parts))])
    whole = lax.all_to_all(payload, "dp", 2, 1, tiled=True)
    hat, upstream, delta, inner = whole[0:2], whole[2:4], whole[4:6], whole[6:8]
    sum_in = jnp.einsum("crd,crh->cdh", hat, delta, preferred_element_type=f32)
    sum_out = jnp.einsum("crh,crd->chd", inner, upstream, preferred_element_type=f32)
    mirror = [(s, sections - 1 - s) for s in range(sections)]
    share = lax.ppermute(jnp.stack([sum_in[1], sum_out[1]]).astype(bf16), "section", mirror)
    total = sum_in[0] + share[0].astype(f32)
    start = lax.axis_index("dp") * branch
    own_gain = lax.dynamic_slice_in_dim(gain[0], start, branch, 0)
    own_in = lax.dynamic_slice_in_dim(w_in[0], start, branch, 0).astype(f32)
    grad_in = total * own_gain[:, None]
    grad_gain = jnp.sum(total * own_in, axis=1)
    grad_out = sum_out[0] + share[1].astype(f32)
    return (grad_in[None], grad_out[None], grad_gain[None])


def solution(mesh):
    return jax.shard_map(
        on_device,
        mesh=mesh,
        in_specs=(
            P(None, "dp", None),
            P(None, "dp", None),
            P("section", None, None),
            P("section", None, None),
            P("section", None),
        ),
        out_specs=(P("section", "dp", None), P("section", None, "dp"), P("section", "dp")),
        check_vma=False,
    )
```

```python
import functools

import jax
import jax.numpy as jnp
from jax import lax
from jax.experimental import pallas as pl
from jax.experimental.pallas import tpu as pltpu
from jax.sharding import PartitionSpec as P

epsilon = 1e-05
STAGES = (0, 1, 2, 3, 2, 1, 0, 1, 2, 3, 2, 1, 0)
LAST = len(STAGES) - 1
MICROS = 2
bf16 = jnp.bfloat16
f32 = jnp.float32
VMEM = pl.BlockSpec(memory_space=pltpu.VMEM)
ANY = pl.BlockSpec(memory_space=pl.ANY)
LOADS = 4
MIB = 2**20


def matmul(left, right):
    return jnp.dot(left, right, preferred_element_type=f32)


def transposed_matmul(left, right):
    return lax.dot_general(left, right, (((0,), (0,)), ((), ())), preferred_element_type=f32)


def place():
    sections = lax.axis_size("section")
    position = lax.axis_index("section")
    half = (position >= sections // 2).astype(jnp.int32)
    fold = jnp.where(half == 0, position, sections - 1 - position)
    return fold, half


def call(body, name, reads, updates=(), places=(), new=(), scratch=(), limit=16):
    n_read, n_update, n_place = len(reads), len(updates), len(places)

    def kernel(*refs):
        ins, outs = refs[: n_read + n_update + n_place], refs[n_read + n_update + n_place :]
        for old, now in zip(ins[n_read : n_read + n_update], outs):
            now[...] = old[...]
        body(ins[:n_read], *outs)

    shapes = [pltpu.VMEM(a.shape, a.dtype) for a in updates]
    shapes += [jax.ShapeDtypeStruct(a.shape, a.dtype) for a in places]
    shapes += list(new)
    kept = [VMEM] * n_update + [ANY] * n_place
    return pl.pallas_call(
        kernel,
        out_shape=tuple(shapes),
        in_specs=[spec for _, spec in reads] + kept,
        out_specs=tuple(kept + [VMEM] * len(new)),
        input_output_aliases={n_read + i: i for i in range(n_update + n_place)},
        scratch_shapes=list(scratch),
        compiler_params=pltpu.CompilerParams(vmem_limit_bytes=limit * MIB),
        cost_estimate=pl.CostEstimate(flops=10**9, bytes_accessed=4 * MIB, transcendentals=0),
        name=name,
    )(*[a for a, _ in reads], *updates, *places)


def load(copy, sources, targets, sems):
    waits = []
    for which, (source, target) in enumerate(zip(sources, targets)):
        size = source.shape[1] // LOADS
        pieces = []
        for i in range(LOADS):
            part = pl.ds(i * size, size)
            pieces.append(
                pltpu.make_async_copy(
                    source.at[copy, part], target.at[part], sems.at[which * LOADS + i]
                )
            )
        for piece in pieces:
            piece.start()
        waits.append(pieces)
    return waits


def wait_all(pieces):
    for piece in pieces:
        piece.wait()


def forward(source, rows, gain, weight_in, weight_out, pack_ref, pre, scale, ready=None):
    chips = pack_ref.shape[0]
    micro, width = source.shape
    chunk = width // chips
    wide = source.astype(f32)
    scaling = lax.rsqrt(jnp.mean(wide * wide, axis=-1, keepdims=True) + epsilon)
    normal = wide * scaling
    if ready is not None:
        wait_all(ready[0])
    before = matmul((normal * gain[...]).astype(bf16), weight_in[...])
    inner = (before * jax.nn.sigmoid(before)).astype(bf16)
    pre[rows, :] = before
    scale[rows, :] = jnp.broadcast_to(scaling, (micro, 128))
    for chip in range(chips):
        pack_ref[chip, :, :chunk] = normal[:, chip * chunk : (chip + 1) * chunk].astype(bf16)
        pack_ref[chip, :, chunk:] = inner
    if ready is not None:
        wait_all(ready[1])
    if weight_out is not None:
        return (wide + matmul(inner, weight_out[...])).astype(bf16)


def backward(grad, rows, gain, weight_in_t, weight_out_t, pack_ref, pre, scale, hats):
    chips = pack_ref.shape[0]
    width = grad.shape[1]
    chunk = width // chips
    before = pre[rows, :]
    sigma = jax.nn.sigmoid(before)
    d_inner = matmul(grad, weight_out_t[...])
    delta = (d_inner * sigma * (1.0 + before * (1.0 - sigma))).astype(bf16)
    for chip in range(chips):
        pack_ref[chip, :, :chunk] = grad[:, chip * chunk : (chip + 1) * chunk]
        pack_ref[chip, :, chunk:] = delta
    if hats is None:
        return None
    mixed = jnp.sum(delta.astype(f32) * before, axis=-1, keepdims=True) / width
    scaled = matmul(delta, weight_in_t[...]) * gain[...]
    scaling = scale[rows, :1]
    result = []
    for chip in range(chips):
        part = slice(chip * chunk, (chip + 1) * chunk)
        normal = hats(chip).astype(f32)
        result.append(
            (grad[:, part].astype(f32) + scaling * (scaled[:, part] - normal * mixed)).astype(bf16)
        )
    return jnp.concatenate(result, axis=1)


def on_device(inputs, cotangent, w_in, w_out, gain):
    sections = lax.axis_size("section")
    parts = lax.axis_size("dp")
    chips = parts // 2
    rows, width = inputs.shape[1:]
    micro = rows // MICROS
    branch = w_in.shape[2]
    chunk = width // chips
    pack = chunk + branch

    dma = pltpu.SemaphoreType.DMA
    block = pltpu.VMEM((micro, width), bf16)
    packed = pltpu.VMEM((chips, micro, pack), bf16)
    in_shape, out_shape = pltpu.VMEM((width, branch), bf16), pltpu.VMEM((branch, width), bf16)
    in_turned, out_turned = out_shape, in_shape
    row_shape = pltpu.VMEM((1, width), f32)
    pre_shapes = (pltpu.VMEM((rows, branch), f32), pltpu.VMEM((rows, 128), f32))
    load_sems = dma((2 * LOADS,))
    same_core = [list(range(core, parts, 2)) for core in range(2)]
    fold_here, _ = place()

    def of_micro(m):
        return pl.ds(m * micro, micro)

    def send_on(sent, stage):
        a, b = STAGES[stage], STAGES[stage + 1]
        pairs = [(a, b), (sections - 1 - a, sections - 1 - b)]
        return lax.ppermute(sent, "section", pairs)

    def exchange(array):
        return lax.all_to_all(array, "dp", 0, 0, axis_index_groups=same_core, tiled=False)

    def new_boxes(name, *layers):
        shapes = [jax.ShapeDtypeStruct((chips, n * rows, pack), bf16) for n in layers]
        return pl.pallas_call(
            lambda *refs: None, out_shape=tuple(shapes), out_specs=(ANY,) * len(shapes), name=name
        )()

    def in_vmem(*arrays):
        return [(a, VMEM) for a in arrays]

    (early,) = new_boxes("early_box", 1)

    def start_kernel(reads, box, sent, weight_in, weight_out, gain_1, gain_2, pre, scale, staged, stash, sem, sems):
        inputs, source_in, source_out, source_gain = reads
        fold, half = place()
        ready = load(half, (source_in, source_out), (weight_in, weight_out), sems)
        gain_1[...] = source_gain[pl.ds(half, 1), :]
        gain_2[...] = source_gain[pl.ds(1 - half, 1), :]

        @pl.when(fold == STAGES[0])
        def _():
            copy = pltpu.make_async_copy(inputs.at[half, of_micro(0)], staged, sem)
            copy.start()
            copy.wait()
            sent[...] = forward(
                staged[...], of_micro(0), gain_1, weight_in, weight_out, stash, pre, scale, ready
            )
            out = pltpu.make_async_copy(stash, box.at[:, of_micro(0), :], sem)
            out.start()
            out.wait()

        @pl.when(fold != STAGES[0])
        def _():
            wait_all(ready[0] + ready[1])

    moved = [None] * MICROS
    early, sent, weight_in, weight_out, gain_1, gain_2, pre_1, scale_1 = call(
        start_kernel,
        "forward_0_0",
        [(inputs, ANY), (w_in, ANY), (w_out, ANY), (gain, VMEM)],
        places=(early,),
        new=(block, in_shape, out_shape, row_shape, row_shape) + pre_shapes,
        scratch=[block, packed, dma(()), load_sems],
        limit=52,
    )
    moved[0] = send_on(sent, 0)
    for m in range(1, MICROS):

        def input_kernel(reads, pre, scale, box, sent, staged, stash, sem, m=m):
            inputs, weight_in, weight_out, gain_1 = reads
            fold, half = place()

            @pl.when(fold == STAGES[0])
            def _():
                copy = pltpu.make_async_copy(inputs.at[half, of_micro(m)], staged, sem)
                copy.start()
                copy.wait()
                sent[...] = forward(
                    staged[...], of_micro(m), gain_1, weight_in, weight_out, stash, pre, scale
                )
                out = pltpu.make_async_copy(stash, box.at[:, of_micro(m), :], sem)
                out.start()
                out.wait()

        pre_1, scale_1, early, sent = call(
            input_kernel,
            "forward_0_%d" % m,
            [(inputs, ANY)] + in_vmem(weight_in, weight_out, gain_1),
            (pre_1, scale_1),
            (early,),
            (block,),
            [block, packed, dma(())],
        )
        moved[m] = send_on(sent, 0)

    def forward_kernel(stage, layer, m, reads, pre, scale, box, sent, stash, sem):
        moved, weight_in, weight_out, gain = reads
        fold, _ = place()

        @pl.when(fold == STAGES[stage])
        def _():
            sent[...] = forward(
                moved[...], of_micro(m), gain, weight_in, weight_out, stash, pre, scale
            )
            out = pltpu.make_async_copy(stash, box.at[:, pl.ds(layer * rows + m * micro, micro), :], sem)
            out.start()
            out.wait()

    def forward_stage(stage, layer, m, weights, kept, box):
        pre, scale, box, sent = call(
            functools.partial(forward_kernel, stage, layer, m),
            "forward_%d_%d" % (stage, m),
            in_vmem(moved[m], *weights),
            kept,
            (box,),
            (block,),
            [packed, dma(())],
        )
        moved[m] = send_on(sent, stage)
        return (pre, scale), box

    kept_1 = (pre_1, scale_1)
    for m in range(MICROS):
        kept_1, early = forward_stage(1, 0, m, (weight_in, weight_out, gain_1), kept_1, early)

    hat_early = lax.cond(fold_here <= 1, exchange, lambda a: a, early)
    (boxes,) = new_boxes("boxes", 2)
    hat_early, boxes, early, gain_1, gain_2, kept_1, w_in, w_out = lax.optimization_barrier(
        (hat_early, boxes, early, gain_1, gain_2, kept_1, w_in, w_out)
    )

    def load_both(reads, *refs):
        weights, (pre, scale), sems = refs[:4], refs[4:6], refs[6:]
        _, half = place()
        waits = load(half, reads, weights[:2], sems[0])
        waits += load(1 - half, reads, weights[2:], sems[1])
        for pieces in waits:
            wait_all(pieces)

    *weights, pre_2, scale_2 = call(
        load_both,
        "load",
        [(w_in, ANY), (w_out, ANY)],
        new=(in_shape, out_shape, in_shape, out_shape) + pre_shapes,
        scratch=[load_sems, load_sems],
        limit=48,
    )
    weights_1, weights_2 = (*weights[:2], gain_1), (*weights[2:], gain_2)
    kept_2 = (pre_2, scale_2)

    for m in range(MICROS):
        kept_1, boxes = forward_stage(2, 0, m, weights_1, kept_1, boxes)

    def turning_kernel(m, reads, pre_1, scale_1, pre_2, scale_2, box, sent, stash, sems):
        moved, in_1, out_1, gain_1, in_2, out_2, gain_2 = reads
        fold, _ = place()

        @pl.when(fold == STAGES[3])
        def _():
            copies = [
                pltpu.make_async_copy(
                    stash.at[i], box.at[:, pl.ds(i * rows + m * micro, micro), :], sems.at[i]
                )
                for i in range(2)
            ]
            sent[...] = forward(
                moved[...], of_micro(m), gain_1, in_1, out_1, stash.at[0], pre_1, scale_1
            )
            copies[0].start()
            sent[...] = forward(
                sent[...], of_micro(m), gain_2, in_2, out_2, stash.at[1], pre_2, scale_2
            )
            copies[1].start()
            wait_all(copies)

    packed_2 = pltpu.VMEM((2, chips, micro, pack), bf16)
    for m in range(MICROS):
        *kept, boxes, sent = call(
            functools.partial(turning_kernel, m),
            "forward_3_%d" % m,
            in_vmem(moved[m], *weights_1, *weights_2),
            kept_1 + kept_2,
            (boxes,),
            (block,),
            [packed_2, dma((2,))],
        )
        kept_1, kept_2 = tuple(kept[:2]), tuple(kept[2:])
        moved[m] = send_on(sent, 3)
    for m in range(MICROS):
        kept_2, boxes = forward_stage(4, 1, m, weights_2, kept_2, boxes)

    def turn(weight_in, weight_out, weight_in_t, weight_out_t):
        @pl.loop(0, width // branch)
        def _(tile):
            part = pl.ds(pl.multiple_of(tile * branch, branch), branch)
            weight_in_t[:, part] = weight_in[part, :].T
            weight_out_t[part, :] = weight_out[:, part].T

    turned_2 = call(
        lambda reads, *refs: turn(*reads, *refs),
        "turn",
        in_vmem(*weights[2:]),
        new=(in_turned, out_turned),
    )
    for m in range(MICROS):
        kept_2, boxes = forward_stage(5, 0, m, weights_2, kept_2, boxes)

    def middle_kernel(m, reads, pre, scale, box, sent, staged, stash, sem, sems):
        moved, cotangent, weight_in, weight_in_t, weight_out_t, gain = reads
        fold, half = place()

        @pl.when(fold == STAGES[6])
        def _():
            copy = pltpu.make_async_copy(cotangent.at[half, of_micro(m)], staged, sem)
            copy.start()
            copies = [
                pltpu.make_async_copy(
                    stash.at[i], box.at[:, pl.ds(i * rows + m * micro, micro), :], sems.at[i]
                )
                for i in range(2)
            ]
            forward(moved[...], of_micro(m), gain, weight_in, None, stash.at[0], pre, scale)
            copies[0].start()
            copy.wait()
            sent[...] = backward(
                staged[...], of_micro(m), gain, weight_in_t, weight_out_t, stash.at[1], pre, scale,
                lambda chip: stash[0, chip, :, :chunk],
            )
            copies[1].start()
            wait_all(copies)

    for m in range(MICROS):
        pre, scale, boxes, sent = call(
            functools.partial(middle_kernel, m),
            "middle_%d" % m,
            [(moved[m], VMEM), (cotangent, ANY)] + in_vmem(weights[2], *turned_2, gain_2),
            kept_2,
            (boxes,),
            (block,),
            [block, packed_2, dma(()), dma((2,))],
        )
        kept_2 = (pre, scale)
        moved[m] = send_on(sent, 6)

    hat_block = pltpu.VMEM((chips, micro, chunk), bf16)

    def fetch(source, layer, m, target, sem):
        source = source.at[:, pl.ds(layer * rows + m * micro, micro), pl.ds(0, chunk)]
        return pltpu.make_async_copy(source, target, sem)

    def backward_kernel(stage, m, hat_layer, layer, reads, box, *refs):
        moved, weight_in_t, weight_out_t, gain, pre, scale = reads[:6]
        sent = refs[0] if stage < LAST else None
        hats, stash, sems = refs[-3:]
        fold, _ = place()

        @pl.when(fold == STAGES[stage])
        def _():
            if sent is not None:
                source = reads[6] if len(reads) > 6 else box
                coming = fetch(source, hat_layer, m, hats, sems.at[0])
                coming.start()

            def normal(chip):
                if chip == 0:
                    coming.wait()
                return hats[chip]

            result = backward(
                moved[...], of_micro(m), gain, weight_in_t, weight_out_t, stash, pre, scale,
                normal if sent is not None else None,
            )
            out = pltpu.make_async_copy(
                stash, box.at[:, pl.ds(layer * rows + m * micro, micro), :], sems.at[1]
            )
            out.start()
            if sent is not None:
                sent[...] = result
            out.wait()

    def backward_stage(stage, m, weights, kept, source, hat_layer, box, layer):
        reads = in_vmem(moved[m], *weights, *kept)
        if source is not None:
            reads.append((source, ANY))
        out = call(
            functools.partial(backward_kernel, stage, m, hat_layer, layer),
            "backward_%d_%d" % (stage, m),
            reads,
            (),
            (box,),
            (block,) if stage < LAST else (),
            [hat_block, packed, dma((2,))],
        )
        if stage < LAST:
            moved[m] = send_on(out[1], stage)
        return out[0]

    for m in range(MICROS):
        boxes = backward_stage(7, m, (*turned_2, gain_2), kept_2, None, 0, boxes, 1)

    both = lax.cond(fold_here < sections, exchange, lambda a: a, boxes)
    late, last = new_boxes("late_boxes", 1, 1)
    both, boxes, late, last, gain_1, gain_2, kept_1, kept_2, early, w_in, w_out = lax.optimization_barrier(
        (both, boxes, late, last, gain_1, gain_2, kept_1, kept_2, early, w_in, w_out)
    )

    def load_turned(reads, in_1, out_1, in_2, out_2, raw_in, raw_out, sems):
        _, half = place()
        for copy, turned in ((half, (in_1, out_1)), (1 - half, (in_2, out_2))):
            waits = load(copy, reads, (raw_in, raw_out), sems)
            wait_all(waits[0] + waits[1])
            turn(raw_in, raw_out, *turned)

    turned = call(
        load_turned,
        "load_turned",
        [(w_in, ANY), (w_out, ANY)],
        new=(in_turned, out_turned, in_turned, out_turned),
        scratch=[in_shape, out_shape, load_sems],
        limit=48,
    )
    turned_1, turned_2 = (*turned[:2], gain_1), (*turned[2:], gain_2)

    for m in range(MICROS):
        late = backward_stage(8, m, turned_2, kept_2, boxes, 1, late, 0)

    def back_turning_kernel(m, reads, late, last, sent, hats, stash, sems):
        moved, in_2, out_2, gain_2, pre_2, scale_2, in_1, out_1, gain_1, pre_1, scale_1, boxes = reads
        fold, _ = place()

        @pl.when(fold == STAGES[9])
        def _():
            coming = [fetch(boxes, layer, m, hats.at[layer], sems.at[layer]) for layer in range(2)]
            for piece in coming:
                piece.start()

            def normal(layer, chip):
                if chip == 0:
                    coming[layer].wait()
                return hats[layer, chip]

            sent[...] = backward(
                moved[...], of_micro(m), gain_2, in_2, out_2, stash.at[0], pre_2, scale_2,
                functools.partial(normal, 1),
            )
            copies = [
                pltpu.make_async_copy(stash.at[i], box.at[:, of_micro(m), :], sems.at[2 + i])
                for i, box in enumerate((late, last))
            ]
            copies[0].start()
            sent[...] = backward(
                sent[...], of_micro(m), gain_1, in_1, out_1, stash.at[1], pre_1, scale_1,
                functools.partial(normal, 0),
            )
            copies[1].start()
            wait_all(copies)

    for m in range(MICROS):
        late, last, sent = call(
            functools.partial(back_turning_kernel, m),
            "backward_9_%d" % m,
            in_vmem(moved[m], *turned_2, *kept_2, *turned_1, *kept_1) + [(boxes, ANY)],
            (),
            (late, last),
            (block,),
            [pltpu.VMEM((2, chips, micro, chunk), bf16), packed_2, dma((4,))],
        )
        moved[m] = send_on(sent, 9)
    for m in range(MICROS):
        last = backward_stage(10, m, turned_1, kept_1, boxes, 0, last, 0)
    for m in range(MICROS):
        late = backward_stage(11, m, turned_1, kept_1, early, 0, late, 0)
    for m in range(MICROS):
        late = backward_stage(LAST, m, turned_1, kept_1, None, 0, late, 0)

    late, last = lax.optimization_barrier((late, last))
    last = lax.cond(fold_here >= 2, exchange, lambda a: a, last)
    late = exchange(late)

    def products(reads, keep, send, whole_in, whole_out):
        early, both, late, last = reads
        fold, half = place()
        core = lax.rem(lax.axis_index("dp"), 2)
        mine = pl.ds(pl.multiple_of(core * branch, branch), branch)
        theirs = pl.ds(pl.multiple_of((1 - core) * branch, branch), branch)

        def product(slot, hat, up):
            def rows_of(ref, part):
                return ref[:, :, part].reshape(chips * rows, -1)

            narrow, wide = slice(chunk, pack), slice(0, chunk)
            whole_in[...] = transposed_matmul(rows_of(hat, wide), rows_of(up, narrow))
            whole_out[...] = transposed_matmul(rows_of(hat, narrow), rows_of(up, wide))
            keep[slot, 0] = whole_in[mine, :]
            keep[slot, 1] = whole_out[:, mine]
            send[slot, 0] = whole_in[theirs, :].astype(bf16)
            send[slot, 1] = whole_out[:, theirs].astype(bf16)

        low, high = both.at[:, :rows], both.at[:, rows:]

        @pl.when(fold <= 1)
        def _():
            product(half, early, late)
            product(1 - half, low, high)

        @pl.when(fold > 1)
        def _():
            product(half, low, last)
            product(1 - half, high, late)

    keep, send = call(
        products,
        "products",
        in_vmem(hat_early, both, late, last),
        new=(pltpu.VMEM((2, 2, branch, branch), f32), pltpu.VMEM((2, 2, branch, branch), bf16)),
        scratch=[pltpu.VMEM((2 * branch, branch), f32), pltpu.VMEM((branch, 2 * branch), f32)],
    )
    total = keep + lax.ppermute(send, "dp", [(i, i ^ 1) for i in range(parts)]).astype(f32)
    mirror = [(s, sections - 1 - s) for s in range(sections)]
    total = total[0] + lax.ppermute(total[1].astype(bf16), "section", mirror).astype(f32)
    start = lax.axis_index("dp") * branch
    own_gain = lax.dynamic_slice_in_dim(gain[0], start, branch, 0)
    own_in = lax.dynamic_slice_in_dim(w_in[0], start, branch, 0).astype(f32)
    grad_in = total[0] * own_gain[:, None]
    grad_gain = jnp.sum(total[0] * own_in, axis=1)
    return (grad_in[None], total[1][None], grad_gain[None])


def solution(mesh):
    return jax.shard_map(
        on_device,
        mesh=mesh,
        in_specs=(
            P(None, "dp", None),
            P(None, "dp", None),
            P("section", None, None),
            P("section", None, None),
            P("section", None),
        ),
        out_specs=(P("section", "dp", None), P("section", None, "dp"), P("section", "dp")),
        check_vma=False,
    )
```

```python
import functools

import jax
import jax.numpy as jnp
from jax import lax
from jax.experimental import pallas as pl
from jax.experimental.pallas import tpu as pltpu
from jax.sharding import PartitionSpec as P

epsilon = 1e-05
STAGES = (0, 1, 2, 3, 2, 1, 0, 1, 2, 3, 2, 1, 0)
LAST = len(STAGES) - 1
MICROS = 2
bf16 = jnp.bfloat16
f32 = jnp.float32
VMEM = pl.BlockSpec(memory_space=pltpu.VMEM)
HBM = pl.BlockSpec(memory_space=pltpu.HBM)
LOADS = 4
MIB = 2**20


def matmul(left, right):
    return jnp.dot(left, right, preferred_element_type=f32)


def transposed_matmul(left, right):
    return lax.dot_general(left, right, (((0,), (0,)), ((), ())), preferred_element_type=f32)


def place():
    sections = lax.axis_size("section")
    position = lax.axis_index("section")
    half = (position >= sections // 2).astype(jnp.int32)
    fold = jnp.where(half == 0, position, sections - 1 - position)
    return fold, half


def call(body, name, reads, updates=(), places=(), new=(), scratch=(), limit=16):
    n_read, n_update, n_place = len(reads), len(updates), len(places)

    def kernel(*refs):
        ins, outs = refs[: n_read + n_update + n_place], refs[n_read + n_update + n_place :]
        for old, now in zip(ins[n_read : n_read + n_update], outs):
            now[...] = old[...]
        body(ins[:n_read], *outs)

    shapes = [pltpu.VMEM(a.shape, a.dtype) for a in updates]
    shapes += [pltpu.HBM(a.shape, a.dtype) for a in places]
    shapes += list(new)
    kept = [VMEM] * n_update + [HBM] * n_place
    return pl.pallas_call(
        kernel,
        out_shape=tuple(shapes),
        in_specs=[spec for _, spec in reads] + kept,
        out_specs=tuple(kept + [VMEM] * len(new)),
        input_output_aliases={n_read + i: i for i in range(n_update + n_place)},
        scratch_shapes=list(scratch),
        compiler_params=pltpu.CompilerParams(vmem_limit_bytes=limit * MIB),
        cost_estimate=pl.CostEstimate(flops=10**9, bytes_accessed=4 * MIB, transcendentals=0),
        name=name,
    )(*[a for a, _ in reads], *updates, *places)


def load(copy, sources, targets, sems):
    waits = []
    for which, (source, target) in enumerate(zip(sources, targets)):
        size = source.shape[1] // LOADS
        pieces = []
        for i in range(LOADS):
            part = pl.ds(i * size, size)
            pieces.append(
                pltpu.make_async_copy(
                    source.at[copy, part], target.at[part], sems.at[which * LOADS + i]
                )
            )
        for piece in pieces:
            piece.start()
        waits.append(pieces)
    return waits


def wait_all(pieces):
    for piece in pieces:
        piece.wait()


def forward(source, gain, weight_in, weight_out, out, ready=None):
    chips = out.rows.shape[0]
    micro, width = source.shape
    branch = weight_in.shape[1]
    chunk = width // chips
    wide = source.astype(f32)
    scaling = lax.rsqrt(jnp.mean(wide * wide, axis=-1, keepdims=True) + epsilon)
    normal = wide * scaling
    if ready is not None:
        wait_all(ready[0])
    before = matmul((normal * gain[...]).astype(bf16), weight_in[...])
    inner = (before * jax.nn.sigmoid(before)).astype(bf16)
    out.kept[:, :branch] = before
    out.kept[:, branch:] = jnp.broadcast_to(scaling, (micro, 128))
    for chip in range(chips):
        out.rows[chip, :, :chunk] = normal[:, chip * chunk : (chip + 1) * chunk].astype(bf16)
        out.rows[chip, :, chunk:] = inner
    out.start()
    if ready is not None:
        wait_all(ready[1])
    if weight_out is not None:
        return (wide + matmul(inner, weight_out[...])).astype(bf16)


def backward(grad, gain, weight_in_t, weight_out_t, out, saved, hats):
    chips = out.rows.shape[0]
    width = grad.shape[1]
    branch = weight_in_t.shape[0]
    chunk = width // chips
    d_inner = matmul(grad, weight_out_t[...])
    kept = saved()
    before = kept[:, :branch]
    sigma = jax.nn.sigmoid(before)
    delta = (d_inner * sigma * (1.0 + before * (1.0 - sigma))).astype(bf16)
    for chip in range(chips):
        out.rows[chip, :, :chunk] = grad[:, chip * chunk : (chip + 1) * chunk]
        out.rows[chip, :, chunk:] = delta
    out.start()
    if hats is None:
        return None
    mixed = jnp.sum(delta.astype(f32) * before, axis=-1, keepdims=True) / width
    scaled = matmul(delta, weight_in_t[...]) * gain[...]
    scaling = kept[:, branch : branch + 1]
    result = []
    for chip in range(chips):
        part = slice(chip * chunk, (chip + 1) * chunk)
        normal = hats(chip).astype(f32)
        result.append(
            (grad[:, part].astype(f32) + scaling * (scaled[:, part] - normal * mixed)).astype(bf16)
        )
    return jnp.concatenate(result, axis=1)


def on_device(inputs, cotangent, w_in, w_out, gain):
    sections = lax.axis_size("section")
    parts = lax.axis_size("dp")
    chips = parts // 2
    rows, width = inputs.shape[1:]
    micro = rows // MICROS
    branch = w_in.shape[2]
    chunk = width // chips
    pack = chunk + branch

    def in_hbm(array):
        return pltpu.with_memory_space_constraint(array, pltpu.HBM)

    raw_in, raw_out = w_in, w_out
    inputs, cotangent, w_in, w_out = map(in_hbm, (inputs, cotangent, w_in, w_out))
    dma = pltpu.SemaphoreType.DMA
    block = pltpu.VMEM((micro, width), bf16)
    packed = pltpu.VMEM((chips, micro, pack), bf16)
    in_shape, out_shape = pltpu.VMEM((width, branch), bf16), pltpu.VMEM((branch, width), bf16)
    in_turned, out_turned = out_shape, in_shape
    row_shape = pltpu.VMEM((1, width), f32)
    load_sems = dma((2 * LOADS,))
    fold_here, _ = place()
    same_core = [list(range(core, parts, 2)) for core in range(2)]

    def of_micro(m):
        return pl.ds(m * micro, micro)

    def send_on(sent, stage):
        a, b = STAGES[stage], STAGES[stage + 1]
        pairs = [(a, b), (sections - 1 - a, sections - 1 - b)]
        return lax.ppermute(sent, "section", pairs)

    def copy_kernel(reads, target, sems):
        copies = [
            pltpu.make_async_copy(reads[0].at[chip], target.at[chip], sems.at[chip])
            for chip in range(chips)
        ]
        for copy in copies:
            copy.start()
        wait_all(copies)

    def exchange(array, keep_in_vmem=False):
        array = lax.all_to_all(array, "dp", 0, 0, axis_index_groups=same_core, tiled=False)
        if keep_in_vmem:
            return array
        array = pltpu.with_memory_space_constraint(array, pltpu.VMEM)
        (target,) = new_boxes("unstage_box", [array.shape])
        (target,) = call(copy_kernel, "unstage", [(array, VMEM)], places=(target,), scratch=[dma((chips,))])
        return target

    def new_boxes(name, shapes):
        shapes = [pltpu.HBM(shape, bf16) for shape in shapes]
        return pl.pallas_call(
            lambda *refs: None, out_shape=tuple(shapes), out_specs=(HBM,) * len(shapes), name=name
        )()

    def in_vmem(*arrays):
        return [(a, VMEM) for a in arrays]

    (box_early,) = new_boxes("box_early", [(chips, rows, pack)])
    box_two, box_far = new_boxes("box_far", [(chips, rows, pack), (chips, 2 * rows, pack)])
    box_near, box_one = new_boxes("box_near", [(chips, 2 * rows, pack), (chips, rows, pack)])
    box_late, box_late_two, box_end = new_boxes(
        "box_late", [(chips, n * rows, pack) for n in (2, 3, 1)]
    )
    (hats,) = new_boxes("hats", [(chips, 2 * rows, chunk)])

    def start_kernel(reads, box, kept, sent, gain, weight_in, weight_out, staged, sem, load_sems, *scratch):
        inputs, source_in, source_out, source_gain = reads
        fold, half = place()

        @pl.when(fold <= 1)
        def _():
            ready = load(half, (source_in, source_out), (weight_in, weight_out), load_sems)
            gain[...] = source_gain[pl.ds(half, 1), :]

            @pl.when(fold == STAGES[0])
            def _():
                copy = pltpu.make_async_copy(inputs.at[half, of_micro(0)], staged, sem)
                copy.start()
                copy.wait()
                out = Keeper(0, scratch, box, layer=0, kept=kept)
                sent[...] = forward(staged[...], gain, weight_in, weight_out, out, ready)
                out.wait()

            @pl.when(fold != STAGES[0])
            def _():
                wait_all(ready[0] + ready[1])

    class Keeper:
        def __init__(self, m, scratch, box, slot=0, layer=0, hats=None, kept=None):
            self.rows, self.kept, sems = scratch
            own = pl.ds(layer * rows + m * micro, micro)
            at = pl.ds(slot * rows + m * micro, micro)
            pairs = [(self.rows, box.at[:, at, :])]
            if hats is not None:
                pairs.append((self.rows.at[:, :, pl.ds(0, chunk)], hats.at[:, own, :]))
            if kept is not None:
                pairs.append((self.kept, kept.at[own, :]))
            self.copies = [
                pltpu.make_async_copy(source, target, sems.at[i])
                for i, (source, target) in enumerate(pairs)
            ]

        def start(self):
            for copy in self.copies:
                copy.start()

        def wait(self):
            wait_all(self.copies)

    kept_shape = pltpu.HBM((2 * rows, branch + 128), f32)
    kept_block = pltpu.VMEM((micro, branch + 128), f32)
    (kept,) = pl.pallas_call(
        lambda *refs: None, out_shape=(kept_shape,), out_specs=(HBM,), name="kept"
    )()

    copies = 3

    def keeping(n=1):
        return [
            pltpu.VMEM((n, chips, micro, pack), bf16),
            pltpu.VMEM((n, micro, branch + 128), f32),
            dma((n, copies)),
        ]

    keeping_one = [packed, kept_block, dma((copies,))]
    moved = [None] * MICROS
    box_early, kept, sent, *weights_1 = call(
        start_kernel,
        "forward_0_0",
        [(inputs, HBM), (w_in, HBM), (w_out, HBM), (gain, VMEM)],
        places=(box_early, kept),
        new=(block, row_shape, in_shape, out_shape),
        scratch=[block, dma(()), load_sems] + keeping_one,
    )
    moved[0] = send_on(sent, 0)
    for m in range(1, MICROS):

        def input_kernel(reads, box, kept, sent, staged, sem, *scratch, m=m):
            inputs, *weights = reads
            fold, half = place()

            @pl.when(fold == STAGES[0])
            def _():
                copy = pltpu.make_async_copy(inputs.at[half, of_micro(m)], staged, sem)
                copy.start()
                copy.wait()
                out = Keeper(m, scratch, box, layer=0, kept=kept)
                sent[...] = forward(staged[...], *weights, out)
                out.wait()

        box_early, kept, sent = call(
            input_kernel,
            "forward_0_%d" % m,
            [(inputs, HBM)] + in_vmem(*weights_1),
            places=(box_early, kept),
            new=(block,),
            scratch=[block, dma(())] + keeping_one,
        )
        moved[m] = send_on(sent, 0)

    def turn(weight_in, weight_out, weight_in_t, weight_out_t):
        @pl.loop(0, width // branch)
        def _(tile):
            part = pl.ds(pl.multiple_of(tile * branch, branch), branch)
            weight_in_t[:, part] = weight_in[part, :].T
            weight_out_t[part, :] = weight_out[:, part].T

    def fresh_weights(name, here, layers, plain, turned):
        def kernel(reads, *refs):
            source_in, source_out, source_gain = reads
            fold, half = place()
            sems, raw = refs[-1], refs[-3:-1]

            @pl.when(here(fold))
            def _():
                waits, at = [], 0
                for i, layer in enumerate(layers):
                    copy = half if layer == 0 else 1 - half
                    gain, *targets = refs[at : at + 1 + 2 * (plain + turned)]
                    at += 1 + 2 * (plain + turned)
                    gain[...] = source_gain[pl.ds(copy, 1), :]
                    loaded = targets[:2] if plain else raw
                    waits.append(load(copy, (source_in, source_out), loaded, sems.at[i]))
                    if turned:
                        wait_all(waits[i][0] + waits[i][1])
                        turn(*loaded, *targets[-2:])
                if not turned:
                    for wait in waits:
                        wait_all(wait[0] + wait[1])

        shapes = (row_shape,) + (in_shape, out_shape) * plain + (in_turned, out_turned) * turned
        outs = call(
            kernel,
            name,
            [(in_hbm(raw_in), HBM), (in_hbm(raw_out), HBM), (gain, VMEM)],
            new=shapes * len(layers),
            scratch=[in_shape, out_shape, dma((len(layers), 2 * LOADS))],
        )
        return [outs[i * len(shapes) : (i + 1) * len(shapes)] for i in range(len(layers))]

    def forward_kernel(stage, slots, m, reads, box, hats, kept, sent, stash, stash_kept, sems):
        moved = reads[0]
        layers = list(slots)
        weights = [reads[1 + 3 * i : 4 + 3 * i] for i in range(len(layers))]
        fold, _ = place()

        @pl.when(fold == STAGES[stage])
        def _():
            outs = [
                Keeper(
                    m,
                    (stash.at[i], stash_kept.at[i], sems.at[i]),
                    box,
                    slot=slots[layer],
                    layer=layer,
                    hats=hats,
                    kept=kept,
                )
                for i, layer in enumerate(layers)
            ]
            for i, out in enumerate(outs):
                source = moved if i == 0 else sent
                sent[...] = forward(source[...], *weights[i], out)
            for out in outs:
                out.wait()

    def forward_stage(stage, slots, box, weights):
        nonlocal hats, kept
        for m in range(MICROS):
            box, hats, kept, sent = call(
                functools.partial(forward_kernel, stage, slots, m),
                "forward_%d_%d" % (stage, m),
                in_vmem(moved[m], *[a for layer in slots for a in weights[layer]]),
                places=(box, hats, kept),
                new=(block,),
                scratch=keeping(len(slots)),
            )
            moved[m] = send_on(sent, stage)
        return box

    box_early = forward_stage(1, {0: 0}, box_early, [weights_1])

    def none(name, array):
        return new_boxes(name, [array.shape])[0]

    box_early, kept = lax.optimization_barrier((box_early, kept))
    got_early = lax.cond(fold_here <= 1, exchange, functools.partial(none, "none_early"), box_early)
    got_early, box_two, box_far, kept, hats, raw_in, raw_out = lax.optimization_barrier(
        (got_early, box_two, box_far, kept, hats, raw_in, raw_out)
    )
    weights = fresh_weights("load_far", lambda fold: fold >= 2, (0, 1), 1, 0)
    box_two = forward_stage(2, {0: 0}, box_two, weights)
    box_far = forward_stage(3, {0: 0, 1: 1}, box_far, weights)
    box_late_two = forward_stage(4, {1: 2}, box_late_two, weights)

    box_two, box_far, kept = lax.optimization_barrier((box_two, box_far, kept))
    got_two, got_far = lax.switch(
        jnp.maximum(fold_here - 1, 0),
        (
            lambda two, far: (none("none_two", two), none("none_far", far)),
            lambda two, far: (exchange(two), none("none_far", far)),
            lambda two, far: (none("none_two", two), exchange(far)),
        ),
        box_two,
        box_far,
    )
    got_two, got_far, box_near, box_one, kept, hats, raw_in, raw_out = lax.optimization_barrier(
        (got_two, got_far, box_near, box_one, kept, hats, raw_in, raw_out)
    )
    (near,) = fresh_weights("load_near", lambda fold: fold <= 1, (1,), 1, 1)
    box_one = forward_stage(5, {1: 0}, box_one, [None, near[:3]])

    def middle_kernel(m, reads, box, kept, sent, staged, sem, stash, stash_kept, sems):
        moved, cotangent, gain, weight_in, weight_in_t, weight_out_t = reads
        fold, half = place()

        @pl.when(fold == STAGES[6])
        def _():
            copy = pltpu.make_async_copy(cotangent.at[half, of_micro(m)], staged, sem)
            copy.start()
            outs = [
                Keeper(m, (stash.at[i], stash_kept.at[0], sems.at[i]), box, slot=i)
                for i in range(2)
            ]
            forward(moved[...], gain, weight_in, None, outs[0])
            copy.wait()
            sent[...] = backward(
                staged[...], gain, weight_in_t, weight_out_t, outs[1], lambda: stash_kept.at[0],
                lambda chip: stash[0, chip, :, :chunk],
            )
            for out in outs:
                out.wait()

    for m in range(MICROS):
        box_near, kept, sent = call(
            functools.partial(middle_kernel, m),
            "middle_%d" % m,
            [(moved[m], VMEM), (cotangent, HBM)] + in_vmem(near[0], near[1], near[3], near[4]),
            places=(box_near, kept),
            new=(block,),
            scratch=[block, dma(())] + keeping(2),
        )
        moved[m] = send_on(sent, 6)

    def saved_rows(name, here, layer):
        def kernel(reads, hats_out, kept_out, sems):
            fold, _ = place()
            at = pl.ds(layer * rows, rows)

            @pl.when(here(fold))
            def _():
                copies = [
                    pltpu.make_async_copy(reads[0].at[chip, at, :], hats_out.at[chip], sems.at[chip])
                    for chip in range(chips)
                ]
                copies.append(pltpu.make_async_copy(reads[1].at[at, :], kept_out, sems.at[chips]))
                for copy in copies:
                    copy.start()
                wait_all(copies)

        return call(
            kernel,
            name,
            [(in_hbm(hats), HBM), (in_hbm(kept), HBM)],
            new=(pltpu.VMEM((chips, rows, chunk), bf16), pltpu.VMEM((rows, branch + 128), f32)),
            scratch=[dma((chips + 1,))],
        )

    def backward_kernel(stage, slots, m, reads, box, kept, *refs):
        moved = reads[0]
        layers = list(slots)
        weights = [reads[1 + 5 * i : 4 + 5 * i] for i in range(len(layers))]
        saved = [reads[4 + 5 * i : 6 + 5 * i] for i in range(len(layers))]
        sent = refs[0] if stage < LAST else None
        stash, stash_kept, sems = refs[-3:]
        fold, _ = place()

        @pl.when(fold == STAGES[stage])
        def _():
            outs = [
                Keeper(m, (stash.at[i], stash_kept.at[i], sems.at[i]), box, slot=slots[layer])
                for i, layer in enumerate(layers)
            ]
            for i, out in enumerate(outs):
                source = moved if i == 0 else sent
                have_hats, have = saved[i]
                result = backward(
                    source[...], *weights[i], out, lambda have=have: have.at[of_micro(m)],
                    (lambda chip, hats=have_hats: hats[chip, of_micro(m), :])
                    if sent is not None
                    else None,
                )
                if sent is not None:
                    sent[...] = result
            for out in outs:
                out.wait()

    def backward_stage(stage, slots, box, weights):
        nonlocal kept
        n = len(slots)
        for m in range(MICROS):
            box, kept, *sent = call(
                functools.partial(backward_kernel, stage, slots, m),
                "backward_%d_%d" % (stage, m),
                in_vmem(moved[m], *[a for layer in slots for a in weights[layer]]) ,
                places=(box, kept),
                new=(block,) if stage < LAST else (),
                scratch=keeping(n),
            )
            if sent:
                moved[m] = send_on(sent[0], stage)
        return box

    saved_2 = saved_rows("saved_near_2", lambda fold: fold == 1, 1)
    box_late = backward_stage(7, {1: 0}, box_late, [None, (near[0], *near[3:], *saved_2)])

    box_near, box_one, kept = lax.optimization_barrier((box_near, box_one, kept))
    got_near, got_one = lax.switch(
        jnp.minimum(fold_here, 2),
        (
            lambda near, one: (exchange(near), none("none_one", one)),
            lambda near, one: (none("none_near", near), exchange(one)),
            lambda near, one: (none("none_near", near), none("none_one", one)),
        ),
        box_near,
        box_one,
    )
    got_near, got_one, box_late, box_late_two, box_end, kept, raw_in, raw_out = lax.optimization_barrier(
        (got_near, got_one, box_late, box_late_two, box_end, kept, raw_in, raw_out)
    )
    (far_2,) = fresh_weights("turn_far_2", lambda fold: fold >= 2, (1,), 0, 1)
    far_2 = (*far_2, *saved_rows("saved_far_2", lambda fold: fold >= 2, 1))
    box_late_two = backward_stage(8, {1: 0}, box_late_two, [None, far_2])
    kept, raw_in, raw_out = lax.optimization_barrier((kept, raw_in, raw_out))
    (far_1,) = fresh_weights("turn_far_1", lambda fold: fold >= 2, (0,), 0, 1)
    far_1 = (*far_1, *saved_rows("saved_far_1", lambda fold: fold >= 2, 0))
    box_late = backward_stage(9, {1: 0, 0: 1}, box_late, [far_1, far_2])
    box_late_two = backward_stage(10, {0: 1}, box_late_two, [far_1])
    kept, raw_in, raw_out = lax.optimization_barrier((kept, raw_in, raw_out))
    (near_1,) = fresh_weights("turn_near_1", lambda fold: fold <= 1, (0,), 0, 1)
    near_1 = (*near_1, *saved_rows("saved_near_1", lambda fold: fold <= 1, 0))
    box_late = backward_stage(11, {0: 1}, box_late, [near_1])
    box_end = backward_stage(LAST, {0: 0}, box_end, [near_1])

    def products(pick, reads, keep, send, whole_in, whole_out):
        _, half = place()
        core = lax.rem(lax.axis_index("dp"), 2)
        mine = pl.ds(pl.multiple_of(core * branch, branch), branch)
        theirs = pl.ds(pl.multiple_of((1 - core) * branch, branch), branch)
        narrow, wide = slice(chunk, pack), slice(0, chunk)

        def part(which, columns):
            box, slot = which
            return reads[box][:, slot * rows : (slot + 1) * rows, columns].reshape(chips * rows, -1)

        for layer, slot in ((0, half), (1, 1 - half)):
            hat, up = pick[layer]
            whole_in[...] = transposed_matmul(part(hat, wide), part(up, narrow))
            whole_out[...] = transposed_matmul(part(hat, narrow), part(up, wide))
            keep[slot, 0] = whole_in[mine, :]
            keep[slot, 1] = whole_out[:, mine]
            send[slot, 0] = whole_in[theirs, :].astype(bf16)
            send[slot, 1] = whole_out[:, theirs].astype(bf16)

    def finish(name, pick, *boxes):
        return call(
            functools.partial(products, pick),
            name,
            in_vmem(*boxes),
            new=(pltpu.VMEM((2, 2, branch, branch), f32), pltpu.VMEM((2, 2, branch, branch), bf16)),
            scratch=[pltpu.VMEM((2 * branch, branch), f32), pltpu.VMEM((branch, 2 * branch), f32)],
        )

    def last(*pick):
        def branch(now, *before):
            arrived = exchange(now, keep_in_vmem=True)
            return finish("products", pick, arrived, *before)

        return branch

    end_0 = last(((1, 0), (0, 0)), ((2, 0), (2, 1)))
    end_1 = last(((1, 0), (0, 1)), ((2, 0), (0, 0)))
    end_2 = last(((1, 0), (0, 1)), ((0, 2), (0, 0)))
    end_3 = last(((1, 0), (0, 1)), ((1, 1), (0, 0)))
    keep, send = lax.switch(
        fold_here,
        (
            lambda end, late, late_two, early, near, one, two, far: end_0(end, early, near),
            lambda end, late, late_two, early, near, one, two, far: end_1(late, early, one),
            lambda end, late, late_two, early, near, one, two, far: end_2(late_two, two),
            lambda end, late, late_two, early, near, one, two, far: end_3(late, far),
        ),
        box_end,
        box_late,
        box_late_two,
        got_early,
        got_near,
        got_one,
        got_two,
        got_far,
    )
    total = keep + lax.ppermute(send, "dp", [(i, i ^ 1) for i in range(parts)]).astype(f32)
    mirror = [(s, sections - 1 - s) for s in range(sections)]
    total = total[0] + lax.ppermute(total[1].astype(bf16), "section", mirror).astype(f32)
    start = lax.axis_index("dp") * branch
    own_gain = lax.dynamic_slice_in_dim(gain[0], start, branch, 0)
    own_in = lax.dynamic_slice_in_dim(raw_in[0], start, branch, 0).astype(f32)
    grad_in = total[0] * own_gain[:, None]
    grad_gain = jnp.sum(total[0] * own_in, axis=1)
    return (grad_in[None], total[1][None], grad_gain[None])


def solution(mesh):
    return jax.shard_map(
        on_device,
        mesh=mesh,
        in_specs=(
            P(None, "dp", None),
            P(None, "dp", None),
            P("section", None, None),
            P("section", None, None),
            P("section", None),
        ),
        out_specs=(P("section", "dp", None), P("section", None, "dp"), P("section", "dp")),
        check_vma=False,
    )
```

```python
import functools

import jax
import jax.numpy as jnp
from jax import lax
from jax.experimental import pallas as pl
from jax.experimental.pallas import tpu as pltpu
from jax.sharding import PartitionSpec as P

epsilon = 1e-05
STAGES = (0, 1, 2, 3, 2, 1, 0, 1, 2, 3, 2, 1, 0)
LAST = len(STAGES) - 1
MICROS = 2
bf16 = jnp.bfloat16
f32 = jnp.float32
VMEM = pl.BlockSpec(memory_space=pltpu.VMEM)
HBM = pl.BlockSpec(memory_space=pltpu.HBM)
LOADS = 4
MIB = 2**20


def matmul(left, right):
    return jnp.dot(left, right, preferred_element_type=f32)


def transposed_matmul(left, right):
    return lax.dot_general(left, right, (((0,), (0,)), ((), ())), preferred_element_type=f32)


def place():
    sections = lax.axis_size("section")
    position = lax.axis_index("section")
    half = (position >= sections // 2).astype(jnp.int32)
    fold = jnp.where(half == 0, position, sections - 1 - position)
    return fold, half


def call(body, name, reads, updates=(), places=(), new=(), scratch=(), limit=16):
    n_read, n_update, n_place = len(reads), len(updates), len(places)

    def kernel(*refs):
        ins, outs = refs[: n_read + n_update + n_place], refs[n_read + n_update + n_place :]
        for old, now in zip(ins[n_read : n_read + n_update], outs):
            now[...] = old[...]
        body(ins[:n_read], *outs)

    shapes = [pltpu.VMEM(a.shape, a.dtype) for a in updates]
    shapes += [pltpu.HBM(a.shape, a.dtype) for a in places]
    shapes += list(new)
    kept = [VMEM] * n_update + [HBM] * n_place
    return pl.pallas_call(
        kernel,
        out_shape=tuple(shapes),
        in_specs=[spec for _, spec in reads] + kept,
        out_specs=tuple(kept + [VMEM] * len(new)),
        input_output_aliases={n_read + i: i for i in range(n_update + n_place)},
        scratch_shapes=list(scratch),
        compiler_params=pltpu.CompilerParams(vmem_limit_bytes=limit * MIB),
        cost_estimate=pl.CostEstimate(flops=1, bytes_accessed=1, transcendentals=0),
        name=name,
    )(*[a for a, _ in reads], *updates, *places)


def load(copy, sources, targets, sems):
    waits = []
    for which, (source, target) in enumerate(zip(sources, targets)):
        size = source.shape[1] // LOADS
        pieces = []
        for i in range(LOADS):
            part = pl.ds(i * size, size)
            pieces.append(
                pltpu.make_async_copy(
                    source.at[copy, part], target.at[part], sems.at[which * LOADS + i]
                )
            )
        for piece in pieces:
            piece.start()
        waits.append(pieces)
    return waits


def wait_all(pieces):
    for piece in pieces:
        piece.wait()


def forward(source, gain, weight_in, weight_out, out, ready=None):
    chips = out.rows.shape[0]
    micro, width = source.shape
    branch = weight_in.shape[1]
    chunk = width // chips
    wide = source.astype(f32)
    scaling = lax.rsqrt(jnp.mean(wide * wide, axis=-1, keepdims=True) + epsilon)
    normal = wide * scaling
    if ready is not None:
        wait_all(ready[0])
    before = matmul((normal * gain[...]).astype(bf16), weight_in[...])
    inner = (before * jax.nn.sigmoid(before)).astype(bf16)
    out.kept[:, :branch] = before
    out.kept[:, branch:] = jnp.broadcast_to(scaling, (micro, 128))
    for chip in range(chips):
        out.rows[chip, :, :chunk] = normal[:, chip * chunk : (chip + 1) * chunk].astype(bf16)
        out.rows[chip, :, chunk:] = inner
    out.start()
    if ready is not None:
        wait_all(ready[1])
    if weight_out is not None:
        return (wide + matmul(inner, weight_out[...])).astype(bf16)


def backward(grad, gain, weight_in_t, weight_out_t, out, saved, hats):
    chips = out.rows.shape[0]
    width = grad.shape[1]
    branch = weight_in_t.shape[0]
    chunk = width // chips
    d_inner = matmul(grad, weight_out_t[...])
    kept = saved()
    before = kept[:, :branch]
    sigma = jax.nn.sigmoid(before)
    delta = (d_inner * sigma * (1.0 + before * (1.0 - sigma))).astype(bf16)
    for chip in range(chips):
        out.rows[chip, :, :chunk] = grad[:, chip * chunk : (chip + 1) * chunk]
        out.rows[chip, :, chunk:] = delta
    out.start()
    if hats is None:
        return None
    mixed = jnp.sum(delta.astype(f32) * before, axis=-1, keepdims=True) / width
    scaled = matmul(delta, weight_in_t[...]) * gain[...]
    scaling = kept[:, branch : branch + 1]
    result = []
    for chip in range(chips):
        part = slice(chip * chunk, (chip + 1) * chunk)
        normal = hats(chip).astype(f32)
        result.append(
            (grad[:, part].astype(f32) + scaling * (scaled[:, part] - normal * mixed)).astype(bf16)
        )
    return jnp.concatenate(result, axis=1)


def on_device(inputs, cotangent, w_in, w_out, gain):
    sections = lax.axis_size("section")
    parts = lax.axis_size("dp")
    chips = parts // 2
    rows, width = inputs.shape[1:]
    micro = rows // MICROS
    branch = w_in.shape[2]
    chunk = width // chips
    pack = chunk + branch

    def in_hbm(array):
        return pltpu.with_memory_space_constraint(array, pltpu.HBM)

    raw_in, raw_out = w_in, w_out
    inputs, cotangent, w_in, w_out = map(in_hbm, (inputs, cotangent, w_in, w_out))
    dma = pltpu.SemaphoreType.DMA
    block = pltpu.VMEM((micro, width), bf16)
    packed = pltpu.VMEM((chips, micro, pack), bf16)
    in_shape, out_shape = pltpu.VMEM((width, branch), bf16), pltpu.VMEM((branch, width), bf16)
    in_turned, out_turned = out_shape, in_shape
    row_shape = pltpu.VMEM((1, width), f32)
    load_sems = dma((2 * LOADS,))
    fold_here, _ = place()
    same_core = [list(range(core, parts, 2)) for core in range(2)]

    def of_micro(m):
        return pl.ds(m * micro, micro)

    def send_on(sent, stage):
        a, b = STAGES[stage], STAGES[stage + 1]
        pairs = [(a, b), (sections - 1 - a, sections - 1 - b)]
        return lax.ppermute(sent, "section", pairs)

    def copy_kernel(reads, target, sems):
        copies = [
            pltpu.make_async_copy(reads[0].at[chip], target.at[chip], sems.at[chip])
            for chip in range(chips)
        ]
        for copy in copies:
            copy.start()
        wait_all(copies)

    def exchange(array, keep_in_vmem=False):
        array = lax.all_to_all(array, "dp", 0, 0, axis_index_groups=same_core, tiled=False)
        if keep_in_vmem:
            return array
        array = pltpu.with_memory_space_constraint(array, pltpu.VMEM)
        (target,) = new_boxes("unstage_box", [array.shape])
        (target,) = call(copy_kernel, "unstage", [(array, VMEM)], places=(target,), scratch=[dma((chips,))])
        return target

    def new_boxes(name, shapes):
        shapes = [pltpu.HBM(shape, bf16) for shape in shapes]
        return pl.pallas_call(
            lambda *refs: None, out_shape=tuple(shapes), out_specs=(HBM,) * len(shapes), name=name
        )()

    def in_vmem(*arrays):
        return [(a, VMEM) for a in arrays]

    (box_early,) = new_boxes("box_early", [(chips, rows, pack)])
    box_two, box_far = new_boxes("box_far", [(chips, rows, pack), (chips, 2 * rows, pack)])
    box_near, box_one = new_boxes("box_near", [(chips, 2 * rows, pack), (chips, rows, pack)])
    box_late, box_late_two, box_end = new_boxes(
        "box_late", [(chips, n * rows, pack) for n in (2, 3, 1)]
    )
    (hats,) = new_boxes("hats", [(chips, 2 * rows, chunk)])

    def start_kernel(reads, box, kept, sent, gain, weight_in, weight_out, staged, sem, load_sems, *scratch):
        inputs, source_in, source_out, source_gain = reads
        fold, half = place()

        @pl.when(fold == STAGES[0])
        def _():
            copy = pltpu.make_async_copy(inputs.at[half, of_micro(0)], staged, sem)
            copy.start()
            ready = load(half, (source_in, source_out), (weight_in, weight_out), load_sems)
            gain[...] = source_gain[pl.ds(half, 1), :]
            copy.wait()
            out = Keeper(0, scratch, box, layer=0, kept=kept)
            sent[...] = forward(staged[...], gain, weight_in, weight_out, out, ready)
            out.wait()

    class Keeper:
        def __init__(self, m, scratch, box, slot=0, layer=0, hats=None, kept=None):
            self.rows, self.kept, sems = scratch
            own = pl.ds(layer * rows + m * micro, micro)
            at = pl.ds(slot * rows + m * micro, micro)
            pairs = [(self.rows, box.at[:, at, :])]
            if hats is not None:
                pairs.append((self.rows.at[:, :, pl.ds(0, chunk)], hats.at[:, own, :]))
            if kept is not None:
                pairs.append((self.kept, kept.at[own, :]))
            self.copies = [
                pltpu.make_async_copy(source, target, sems.at[i])
                for i, (source, target) in enumerate(pairs)
            ]

        def start(self):
            for copy in self.copies:
                copy.start()

        def wait(self):
            wait_all(self.copies)

    kept_shape = pltpu.HBM((2 * rows, branch + 128), f32)
    kept_block = pltpu.VMEM((micro, branch + 128), f32)
    (kept,) = pl.pallas_call(
        lambda *refs: None, out_shape=(kept_shape,), out_specs=(HBM,), name="kept"
    )()

    copies = 3

    def keeping(n=1):
        return [
            pltpu.VMEM((n, chips, micro, pack), bf16),
            pltpu.VMEM((n, micro, branch + 128), f32),
            dma((n, copies)),
        ]

    keeping_one = [packed, kept_block, dma((copies,))]
    moved = [None] * MICROS
    box_early, kept, sent, *weights_1 = call(
        start_kernel,
        "forward_0_0",
        [(inputs, HBM), (w_in, HBM), (w_out, HBM), (gain, VMEM)],
        places=(box_early, kept),
        new=(block, row_shape, in_shape, out_shape),
        scratch=[block, dma(()), load_sems] + keeping_one,
    )
    moved[0] = send_on(sent, 0)
    for m in range(1, MICROS):

        def input_kernel(reads, box, kept, sent, staged, sem, *scratch, m=m):
            inputs, *weights = reads
            fold, half = place()

            @pl.when(fold == STAGES[0])
            def _():
                copy = pltpu.make_async_copy(inputs.at[half, of_micro(m)], staged, sem)
                copy.start()
                copy.wait()
                out = Keeper(m, scratch, box, layer=0, kept=kept)
                sent[...] = forward(staged[...], *weights, out)
                out.wait()

        box_early, kept, sent = call(
            input_kernel,
            "forward_0_%d" % m,
            [(inputs, HBM)] + in_vmem(*weights_1),
            places=(box_early, kept),
            new=(block,),
            scratch=[block, dma(())] + keeping_one,
        )
        moved[m] = send_on(sent, 0)

    def turn(weight_in, weight_out, weight_in_t, weight_out_t):
        @pl.loop(0, width // branch)
        def _(tile):
            part = pl.ds(pl.multiple_of(tile * branch, branch), branch)
            weight_in_t[:, part] = weight_in[part, :].T
            weight_out_t[part, :] = weight_out[:, part].T

    def fresh_weights(name, here, layers, plain, turned):
        def kernel(reads, *refs):
            source_in, source_out, source_gain = reads
            fold, half = place()
            sems, raw = refs[-1], refs[-3:-1]

            @pl.when(here(fold))
            def _():
                waits, at = [], 0
                for i, layer in enumerate(layers):
                    copy = half if layer == 0 else 1 - half
                    gain, *targets = refs[at : at + 1 + 2 * (plain + turned)]
                    at += 1 + 2 * (plain + turned)
                    gain[...] = source_gain[pl.ds(copy, 1), :]
                    loaded = targets[:2] if plain else raw
                    waits.append(load(copy, (source_in, source_out), loaded, sems.at[i]))
                    if turned:
                        wait_all(waits[i][0] + waits[i][1])
                        turn(*loaded, *targets[-2:])
                if not turned:
                    for wait in waits:
                        wait_all(wait[0] + wait[1])

        shapes = (row_shape,) + (in_shape, out_shape) * plain + (in_turned, out_turned) * turned
        outs = call(
            kernel,
            name,
            [(in_hbm(raw_in), HBM), (in_hbm(raw_out), HBM), (gain, VMEM)],
            new=shapes * len(layers),
            scratch=[in_shape, out_shape, dma((len(layers), 2 * LOADS))],
        )
        return [outs[i * len(shapes) : (i + 1) * len(shapes)] for i in range(len(layers))]

    def forward_kernel(stage, slots, m, reads, box, hats, kept, sent, stash, stash_kept, sems):
        moved = reads[0]
        layers = list(slots)
        weights = [reads[1 + 3 * i : 4 + 3 * i] for i in range(len(layers))]
        fold, _ = place()

        @pl.when(fold == STAGES[stage])
        def _():
            outs = [
                Keeper(
                    m,
                    (stash.at[i], stash_kept.at[i], sems.at[i]),
                    box,
                    slot=slots[layer],
                    layer=layer,
                    hats=hats,
                    kept=kept,
                )
                for i, layer in enumerate(layers)
            ]
            for i, out in enumerate(outs):
                source = moved if i == 0 else sent
                sent[...] = forward(source[...], *weights[i], out)
            for out in outs:
                out.wait()

    def forward_stage(stage, slots, box, weights):
        nonlocal hats, kept
        for m in range(MICROS):
            box, hats, kept, sent = call(
                functools.partial(forward_kernel, stage, slots, m),
                "forward_%d_%d" % (stage, m),
                in_vmem(moved[m], *[a for layer in slots for a in weights[layer]]),
                places=(box, hats, kept),
                new=(block,),
                scratch=keeping(len(slots)),
            )
            moved[m] = send_on(sent, stage)
        return box

    weights = fresh_weights("load_1", lambda fold: fold == 1, (0,), 1, 0)
    box_early = forward_stage(1, {0: 0}, box_early, weights)

    def none(name, array):
        return new_boxes(name, [array.shape])[0]

    box_early, kept = lax.optimization_barrier((box_early, kept))
    got_early = lax.cond(fold_here <= 1, exchange, functools.partial(none, "none_early"), box_early)
    got_early, box_two, box_far, kept, hats, raw_in, raw_out = lax.optimization_barrier(
        (got_early, box_two, box_far, kept, hats, raw_in, raw_out)
    )
    weights = fresh_weights("load_2", lambda fold: fold == 2, (0,), 1, 0)
    box_two = forward_stage(2, {0: 0}, box_two, weights)
    raw_in, raw_out, kept = lax.optimization_barrier((raw_in, raw_out, kept))
    weights = fresh_weights("load_3", lambda fold: fold == 3, (0, 1), 1, 0)
    box_far = forward_stage(3, {0: 0, 1: 1}, box_far, weights)
    raw_in, raw_out, kept = lax.optimization_barrier((raw_in, raw_out, kept))
    weights = fresh_weights("load_4", lambda fold: fold == 2, (1,), 1, 0)
    box_late_two = forward_stage(4, {1: 2}, box_late_two, [None, *weights])

    box_two, box_far, kept = lax.optimization_barrier((box_two, box_far, kept))
    got_two, got_far = lax.switch(
        jnp.maximum(fold_here - 1, 0),
        (
            lambda two, far: (none("none_two", two), none("none_far", far)),
            lambda two, far: (exchange(two), none("none_far", far)),
            lambda two, far: (none("none_two", two), exchange(far)),
        ),
        box_two,
        box_far,
    )
    got_two, got_far, box_near, box_one, kept, hats, raw_in, raw_out = lax.optimization_barrier(
        (got_two, got_far, box_near, box_one, kept, hats, raw_in, raw_out)
    )
    (near,) = fresh_weights("load_near", lambda fold: fold <= 1, (1,), 1, 1)
    box_one = forward_stage(5, {1: 0}, box_one, [None, near[:3]])

    def middle_kernel(m, reads, box, kept, sent, staged, sem, stash, stash_kept, sems):
        moved, cotangent, gain, weight_in, weight_in_t, weight_out_t = reads
        fold, half = place()

        @pl.when(fold == STAGES[6])
        def _():
            copy = pltpu.make_async_copy(cotangent.at[half, of_micro(m)], staged, sem)
            copy.start()
            outs = [
                Keeper(m, (stash.at[i], stash_kept.at[0], sems.at[i]), box, slot=i)
                for i in range(2)
            ]
            forward(moved[...], gain, weight_in, None, outs[0])
            copy.wait()
            sent[...] = backward(
                staged[...], gain, weight_in_t, weight_out_t, outs[1], lambda: stash_kept.at[0],
                lambda chip: stash[0, chip, :, :chunk],
            )
            for out in outs:
                out.wait()

    for m in range(MICROS):
        box_near, kept, sent = call(
            functools.partial(middle_kernel, m),
            "middle_%d" % m,
            [(moved[m], VMEM), (cotangent, HBM)] + in_vmem(near[0], near[1], near[3], near[4]),
            places=(box_near, kept),
            new=(block,),
            scratch=[block, dma(())] + keeping(2),
        )
        moved[m] = send_on(sent, 6)

    def saved_rows(name, here, layer):
        def kernel(reads, hats_out, kept_out, sems):
            fold, _ = place()
            at = pl.ds(layer * rows, rows)

            @pl.when(here(fold))
            def _():
                copies = [
                    pltpu.make_async_copy(reads[0].at[chip, at, :], hats_out.at[chip], sems.at[chip])
                    for chip in range(chips)
                ]
                copies.append(pltpu.make_async_copy(reads[1].at[at, :], kept_out, sems.at[chips]))
                for copy in copies:
                    copy.start()
                wait_all(copies)

        return call(
            kernel,
            name,
            [(in_hbm(hats), HBM), (in_hbm(kept), HBM)],
            new=(pltpu.VMEM((chips, rows, chunk), bf16), pltpu.VMEM((rows, branch + 128), f32)),
            scratch=[dma((chips + 1,))],
        )

    def backward_kernel(stage, slots, m, reads, box, kept, *refs):
        moved = reads[0]
        layers = list(slots)
        weights = [reads[1 + 5 * i : 4 + 5 * i] for i in range(len(layers))]
        saved = [reads[4 + 5 * i : 6 + 5 * i] for i in range(len(layers))]
        sent = refs[0] if stage < LAST else None
        stash, stash_kept, sems = refs[-3:]
        fold, _ = place()

        @pl.when(fold == STAGES[stage])
        def _():
            outs = [
                Keeper(m, (stash.at[i], stash_kept.at[i], sems.at[i]), box, slot=slots[layer])
                for i, layer in enumerate(layers)
            ]
            for i, out in enumerate(outs):
                source = moved if i == 0 else sent
                have_hats, have = saved[i]
                result = backward(
                    source[...], *weights[i], out, lambda have=have: have.at[of_micro(m)],
                    (lambda chip, hats=have_hats: hats[chip, of_micro(m), :])
                    if sent is not None
                    else None,
                )
                if sent is not None:
                    sent[...] = result
            for out in outs:
                out.wait()

    def backward_stage(stage, slots, box, weights):
        nonlocal kept
        n = len(slots)
        for m in range(MICROS):
            box, kept, *sent = call(
                functools.partial(backward_kernel, stage, slots, m),
                "backward_%d_%d" % (stage, m),
                in_vmem(moved[m], *[a for layer in slots for a in weights[layer]]) ,
                places=(box, kept),
                new=(block,) if stage < LAST else (),
                scratch=keeping(n),
            )
            if sent:
                moved[m] = send_on(sent[0], stage)
        return box

    saved_2 = saved_rows("saved_near_2", lambda fold: fold == 1, 1)
    box_late = backward_stage(7, {1: 0}, box_late, [None, (near[0], *near[3:], *saved_2)])

    box_near, box_one, kept = lax.optimization_barrier((box_near, box_one, kept))
    got_near, got_one = lax.switch(
        jnp.minimum(fold_here, 2),
        (
            lambda near, one: (exchange(near), none("none_one", one)),
            lambda near, one: (none("none_near", near), exchange(one)),
            lambda near, one: (none("none_near", near), none("none_one", one)),
        ),
        box_near,
        box_one,
    )
    got_near, got_one, box_late, box_late_two, box_end, kept, raw_in, raw_out = lax.optimization_barrier(
        (got_near, got_one, box_late, box_late_two, box_end, kept, raw_in, raw_out)
    )
    (far_2,) = fresh_weights("turn_far_2", lambda fold: fold >= 2, (1,), 0, 1)
    far_2 = (*far_2, *saved_rows("saved_far_2", lambda fold: fold >= 2, 1))
    box_late_two = backward_stage(8, {1: 0}, box_late_two, [None, far_2])
    kept, raw_in, raw_out = lax.optimization_barrier((kept, raw_in, raw_out))
    (far_1,) = fresh_weights("turn_far_1", lambda fold: fold >= 2, (0,), 0, 1)
    far_1 = (*far_1, *saved_rows("saved_far_1", lambda fold: fold >= 2, 0))
    box_late = backward_stage(9, {1: 0, 0: 1}, box_late, [far_1, far_2])
    box_late_two = backward_stage(10, {0: 1}, box_late_two, [far_1])
    kept, raw_in, raw_out = lax.optimization_barrier((kept, raw_in, raw_out))
    (near_1,) = fresh_weights("turn_11", lambda fold: fold == 1, (0,), 0, 1)
    near_1 = (*near_1, *saved_rows("saved_11", lambda fold: fold == 1, 0))
    box_late = backward_stage(11, {0: 1}, box_late, [near_1])
    kept, raw_in, raw_out = lax.optimization_barrier((kept, raw_in, raw_out))
    (near_1,) = fresh_weights("turn_12", lambda fold: fold == 0, (0,), 0, 1)
    near_1 = (*near_1, *saved_rows("saved_12", lambda fold: fold == 0, 0))
    box_end = backward_stage(LAST, {0: 0}, box_end, [near_1])

    def products(pick, reads, keep, send, whole_in, whole_out):
        _, half = place()
        core = lax.rem(lax.axis_index("dp"), 2)
        mine = pl.ds(pl.multiple_of(core * branch, branch), branch)
        theirs = pl.ds(pl.multiple_of((1 - core) * branch, branch), branch)
        narrow, wide = slice(chunk, pack), slice(0, chunk)

        def part(which, columns):
            box, slot = which
            return reads[box][:, slot * rows : (slot + 1) * rows, columns].reshape(chips * rows, -1)

        for layer, slot in ((0, half), (1, 1 - half)):
            hat, up = pick[layer]
            whole_in[...] = transposed_matmul(part(hat, wide), part(up, narrow))
            whole_out[...] = transposed_matmul(part(hat, narrow), part(up, wide))
            keep[slot, 0] = whole_in[mine, :]
            keep[slot, 1] = whole_out[:, mine]
            send[slot, 0] = whole_in[theirs, :].astype(bf16)
            send[slot, 1] = whole_out[:, theirs].astype(bf16)

    def finish(name, pick, *boxes):
        return call(
            functools.partial(products, pick),
            name,
            in_vmem(*boxes),
            new=(pltpu.VMEM((2, 2, branch, branch), f32), pltpu.VMEM((2, 2, branch, branch), bf16)),
            scratch=[pltpu.VMEM((2 * branch, branch), f32), pltpu.VMEM((branch, 2 * branch), f32)],
        )

    def last(*pick):
        def branch(now, *before):
            arrived = exchange(now, keep_in_vmem=True)
            return finish("products", pick, arrived, *before)

        return branch

    end_0 = last(((1, 0), (0, 0)), ((2, 0), (2, 1)))
    end_1 = last(((1, 0), (0, 1)), ((2, 0), (0, 0)))
    end_2 = last(((1, 0), (0, 1)), ((0, 2), (0, 0)))
    end_3 = last(((1, 0), (0, 1)), ((1, 1), (0, 0)))
    keep, send = lax.switch(
        fold_here,
        (
            lambda end, late, late_two, early, near, one, two, far: end_0(end, early, near),
            lambda end, late, late_two, early, near, one, two, far: end_1(late, early, one),
            lambda end, late, late_two, early, near, one, two, far: end_2(late_two, two),
            lambda end, late, late_two, early, near, one, two, far: end_3(late, far),
        ),
        box_end,
        box_late,
        box_late_two,
        got_early,
        got_near,
        got_one,
        got_two,
        got_far,
    )
    total = keep + lax.ppermute(send, "dp", [(i, i ^ 1) for i in range(parts)]).astype(f32)
    mirror = [(s, sections - 1 - s) for s in range(sections)]
    total = total[0] + lax.ppermute(total[1].astype(bf16), "section", mirror).astype(f32)
    start = lax.axis_index("dp") * branch
    own_gain = lax.dynamic_slice_in_dim(gain[0], start, branch, 0)
    own_in = lax.dynamic_slice_in_dim(raw_in[0], start, branch, 0).astype(f32)
    grad_in = total[0] * own_gain[:, None]
    grad_gain = jnp.sum(total[0] * own_in, axis=1)
    return (grad_in[None], total[1][None], grad_gain[None])


def solution(mesh):
    return jax.shard_map(
        on_device,
        mesh=mesh,
        in_specs=(
            P(None, "dp", None),
            P(None, "dp", None),
            P("section", None, None),
            P("section", None, None),
            P("section", None),
        ),
        out_specs=(P("section", "dp", None), P("section", None, "dp"), P("section", "dp")),
        check_vma=False,
    )
```

```python
import functools

import jax
import jax.numpy as jnp
from jax import lax
from jax.experimental import pallas as pl
from jax.experimental.pallas import tpu as pltpu
from jax.sharding import PartitionSpec as P

epsilon = 1e-05
STAGES = (0, 1, 2, 3, 2, 1, 0, 1, 2, 3, 2, 1, 0)
LAST = len(STAGES) - 1
MICROS = 2
bf16 = jnp.bfloat16
f32 = jnp.float32
VMEM = pl.BlockSpec(memory_space=pltpu.VMEM)
HBM = pl.BlockSpec(memory_space=pltpu.HBM)
LOADS = 4
MIB = 2**20


def matmul(left, right):
    return jnp.dot(left, right, preferred_element_type=f32)


def transposed_matmul(left, right):
    return lax.dot_general(left, right, (((0,), (0,)), ((), ())), preferred_element_type=f32)


def place():
    sections = lax.axis_size("section")
    position = lax.axis_index("section")
    half = (position >= sections // 2).astype(jnp.int32)
    fold = jnp.where(half == 0, position, sections - 1 - position)
    return fold, half


def call(body, name, reads, updates=(), places=(), new=(), scratch=(), limit=16):
    n_read, n_update, n_place = len(reads), len(updates), len(places)

    def kernel(*refs):
        ins, outs = refs[: n_read + n_update + n_place], refs[n_read + n_update + n_place :]
        for old, now in zip(ins[n_read : n_read + n_update], outs):
            now[...] = old[...]
        body(ins[:n_read], *outs)

    shapes = [pltpu.VMEM(a.shape, a.dtype) for a in updates]
    shapes += [pltpu.HBM(a.shape, a.dtype) for a in places]
    shapes += list(new)
    kept = [VMEM] * n_update + [HBM] * n_place
    return pl.pallas_call(
        kernel,
        out_shape=tuple(shapes),
        in_specs=[spec for _, spec in reads] + kept,
        out_specs=tuple(kept + [VMEM] * len(new)),
        input_output_aliases={n_read + i: i for i in range(n_update + n_place)},
        scratch_shapes=list(scratch),
        compiler_params=pltpu.CompilerParams(vmem_limit_bytes=limit * MIB),
        cost_estimate=pl.CostEstimate(flops=1, bytes_accessed=1, transcendentals=0),
        name=name,
    )(*[a for a, _ in reads], *updates, *places)


def load(copy, sources, targets, sems):
    waits = []
    for which, (source, target) in enumerate(zip(sources, targets)):
        size = source.shape[1] // LOADS
        pieces = []
        for i in range(LOADS):
            part = pl.ds(i * size, size)
            pieces.append(
                pltpu.make_async_copy(
                    source.at[copy, part], target.at[part], sems.at[which * LOADS + i]
                )
            )
        for piece in pieces:
            piece.start()
        waits.append(pieces)
    return waits


def wait_all(pieces):
    for piece in pieces:
        piece.wait()


def forward(source, gain, weight_in, weight_out, out, ready=None):
    chips = out.rows.shape[0]
    micro, width = source.shape
    branch = weight_in.shape[1]
    chunk = width // chips
    wide = source.astype(f32)
    scaling = lax.rsqrt(jnp.mean(wide * wide, axis=-1, keepdims=True) + epsilon)
    normal = wide * scaling
    if ready is not None:
        wait_all(ready[0])
    before = matmul((normal * gain[...]).astype(bf16), weight_in[...])
    inner = (before * jax.nn.sigmoid(before)).astype(bf16)
    out.kept[:, :branch] = before
    out.kept[:, branch:] = jnp.broadcast_to(scaling, (micro, 128))
    for chip in range(chips):
        out.rows[chip, :, :chunk] = normal[:, chip * chunk : (chip + 1) * chunk].astype(bf16)
        out.rows[chip, :, chunk:] = inner
    out.start()
    if ready is not None:
        wait_all(ready[1])
    if weight_out is not None:
        return (wide + matmul(inner, weight_out[...])).astype(bf16)


def backward(grad, gain, weight_in_t, weight_out_t, out, saved, hats):
    chips = out.rows.shape[0]
    width = grad.shape[1]
    branch = weight_in_t.shape[0]
    chunk = width // chips
    d_inner = matmul(grad, weight_out_t[...])
    kept = saved()
    before = kept[:, :branch]
    sigma = jax.nn.sigmoid(before)
    delta = (d_inner * sigma * (1.0 + before * (1.0 - sigma))).astype(bf16)
    for chip in range(chips):
        out.rows[chip, :, :chunk] = grad[:, chip * chunk : (chip + 1) * chunk]
        out.rows[chip, :, chunk:] = delta
    out.start()
    if hats is None:
        return None
    mixed = jnp.sum(delta.astype(f32) * before, axis=-1, keepdims=True) / width
    scaled = matmul(delta, weight_in_t[...]) * gain[...]
    scaling = kept[:, branch : branch + 1]
    result = []
    for chip in range(chips):
        part = slice(chip * chunk, (chip + 1) * chunk)
        normal = hats(chip).astype(f32)
        result.append(
            (grad[:, part].astype(f32) + scaling * (scaled[:, part] - normal * mixed)).astype(bf16)
        )
    return jnp.concatenate(result, axis=1)


def on_device(inputs, cotangent, w_in, w_out, gain):
    sections = lax.axis_size("section")
    parts = lax.axis_size("dp")
    chips = parts // 2
    rows, width = inputs.shape[1:]
    micro = rows // MICROS
    branch = w_in.shape[2]
    chunk = width // chips
    pack = chunk + branch

    def in_hbm(array):
        return pltpu.with_memory_space_constraint(array, pltpu.HBM)

    raw_in, raw_out = w_in, w_out
    inputs, cotangent, w_in, w_out = map(in_hbm, (inputs, cotangent, w_in, w_out))
    dma = pltpu.SemaphoreType.DMA
    block = pltpu.VMEM((micro, width), bf16)
    packed = pltpu.VMEM((chips, micro, pack), bf16)
    in_shape, out_shape = pltpu.VMEM((width, branch), bf16), pltpu.VMEM((branch, width), bf16)
    in_turned, out_turned = out_shape, in_shape
    row_shape = pltpu.VMEM((1, width), f32)
    load_sems = dma((2 * LOADS,))
    fold_here, _ = place()
    same_core = [list(range(core, parts, 2)) for core in range(2)]

    def of_micro(m):
        return pl.ds(m * micro, micro)

    def send_on(sent, stage):
        a, b = STAGES[stage], STAGES[stage + 1]
        pairs = [(a, b), (sections - 1 - a, sections - 1 - b)]
        return lax.ppermute(sent, "section", pairs)

    def copy_kernel(reads, target, sems):
        copies = [
            pltpu.make_async_copy(reads[0].at[chip], target.at[chip], sems.at[chip])
            for chip in range(chips)
        ]
        for copy in copies:
            copy.start()
        wait_all(copies)

    def exchange(array, raw=False):
        array = lax.all_to_all(array, "dp", 0, 0, axis_index_groups=same_core, tiled=False)
        if raw:
            return array
        array = pltpu.with_memory_space_constraint(array, pltpu.VMEM)
        (target,) = new_boxes("unstage_box", [array.shape])
        (target,) = call(copy_kernel, "unstage", [(array, VMEM)], places=(target,), scratch=[dma((chips,))])
        return target

    def new_boxes(name, shapes):
        shapes = [pltpu.HBM(shape, bf16) for shape in shapes]
        return pl.pallas_call(
            lambda *refs: None, out_shape=tuple(shapes), out_specs=(HBM,) * len(shapes), name=name
        )()

    def in_vmem(*arrays):
        return [(a, VMEM) for a in arrays]

    (box_early,) = new_boxes("box_early", [(chips, rows, pack)])
    (box_two,) = new_boxes("box_two", [(chips, rows, pack)])
    box_near, box_one = new_boxes("box_near", [(chips, 2 * rows, pack), (chips, rows, pack)])
    box_late, box_late_two, box_end = new_boxes(
        "box_late", [(chips, n * rows, pack) for n in (2, 3, 1)]
    )
    (hats,) = new_boxes("hats", [(chips, 2 * rows, chunk)])

    def start_kernel(reads, box, kept, sent, gain, weight_in, weight_out, staged, sem, load_sems, *scratch):
        inputs, source_in, source_out, source_gain = reads
        fold, half = place()

        @pl.when(fold == STAGES[0])
        def _():
            copy = pltpu.make_async_copy(inputs.at[half, of_micro(0)], staged, sem)
            copy.start()
            ready = load(half, (source_in, source_out), (weight_in, weight_out), load_sems)
            gain[...] = source_gain[pl.ds(half, 1), :]
            copy.wait()
            out = Keeper(0, scratch, box, layer=0, kept=kept)
            sent[...] = forward(staged[...], gain, weight_in, weight_out, out, ready)
            out.wait()

    class Keeper:
        def __init__(self, m, scratch, box, slot=0, layer=0, hats=None, kept=None):
            self.rows, self.kept, sems = scratch
            own = pl.ds(layer * rows + m * micro, micro)
            at = pl.ds(slot * rows + m * micro, micro)
            pairs = [(self.rows, box.at[:, at, :])]
            if hats is not None:
                pairs.append((self.rows.at[:, :, pl.ds(0, chunk)], hats.at[:, own, :]))
            if kept is not None:
                pairs.append((self.kept, kept.at[own, :]))
            self.copies = [
                pltpu.make_async_copy(source, target, sems.at[i])
                for i, (source, target) in enumerate(pairs)
            ]

        def start(self):
            for copy in self.copies:
                copy.start()

        def wait(self):
            wait_all(self.copies)

    kept_shape = pltpu.HBM((2 * rows, branch + 128), f32)
    kept_block = pltpu.VMEM((micro, branch + 128), f32)
    (kept,) = pl.pallas_call(
        lambda *refs: None, out_shape=(kept_shape,), out_specs=(HBM,), name="kept"
    )()

    copies = 3

    def keeping(n=1):
        return [
            pltpu.VMEM((n, chips, micro, pack), bf16),
            pltpu.VMEM((n, micro, branch + 128), f32),
            dma((n, copies)),
        ]

    keeping_one = [packed, kept_block, dma((copies,))]
    moved = [None] * MICROS
    box_early, kept, sent, *weights_1 = call(
        start_kernel,
        "forward_0_0",
        [(inputs, HBM), (w_in, HBM), (w_out, HBM), (gain, VMEM)],
        places=(box_early, kept),
        new=(block, row_shape, in_shape, out_shape),
        scratch=[block, dma(()), load_sems] + keeping_one,
    )
    moved[0] = send_on(sent, 0)
    for m in range(1, MICROS):

        def input_kernel(reads, box, kept, sent, staged, sem, *scratch, m=m):
            inputs, *weights = reads
            fold, half = place()

            @pl.when(fold == STAGES[0])
            def _():
                copy = pltpu.make_async_copy(inputs.at[half, of_micro(m)], staged, sem)
                copy.start()
                copy.wait()
                out = Keeper(m, scratch, box, layer=0, kept=kept)
                sent[...] = forward(staged[...], *weights, out)
                out.wait()

        box_early, kept, sent = call(
            input_kernel,
            "forward_0_%d" % m,
            [(inputs, HBM)] + in_vmem(*weights_1),
            places=(box_early, kept),
            new=(block,),
            scratch=[block, dma(())] + keeping_one,
        )
        moved[m] = send_on(sent, 0)

    def turn(weight_in, weight_out, weight_in_t, weight_out_t):
        @pl.loop(0, width // branch)
        def _(tile):
            part = pl.ds(pl.multiple_of(tile * branch, branch), branch)
            weight_in_t[:, part] = weight_in[part, :].T
            weight_out_t[part, :] = weight_out[:, part].T

    def fresh_weights(name, here, layers, plain, turned):
        def kernel(reads, *refs):
            source_in, source_out, source_gain = reads
            fold, half = place()
            sems, raw = refs[-1], refs[-3:-1]

            @pl.when(here(fold))
            def _():
                waits, at = [], 0
                for i, layer in enumerate(layers):
                    copy = half if layer == 0 else 1 - half
                    gain, *targets = refs[at : at + 1 + 2 * (plain + turned)]
                    at += 1 + 2 * (plain + turned)
                    gain[...] = source_gain[pl.ds(copy, 1), :]
                    loaded = targets[:2] if plain else raw
                    waits.append(load(copy, (source_in, source_out), loaded, sems.at[i]))
                    if turned:
                        wait_all(waits[i][0] + waits[i][1])
                        turn(*loaded, *targets[-2:])
                if not turned:
                    for wait in waits:
                        wait_all(wait[0] + wait[1])

        shapes = (row_shape,) + (in_shape, out_shape) * plain + (in_turned, out_turned) * turned
        outs = call(
            kernel,
            name,
            [(in_hbm(raw_in), HBM), (in_hbm(raw_out), HBM), (gain, VMEM)],
            new=shapes * len(layers),
            scratch=[in_shape, out_shape, dma((len(layers), 2 * LOADS))],
        )
        return [outs[i * len(shapes) : (i + 1) * len(shapes)] for i in range(len(layers))]

    def forward_kernel(stage, slots, m, reads, *refs):
        moved = reads[0]
        boxes, (hats, kept, sent, stash, stash_kept, sems) = refs[:-6], refs[-6:]
        layers = list(slots)
        weights = [reads[1 + 3 * i : 4 + 3 * i] for i in range(len(layers))]
        fold, _ = place()

        @pl.when(fold == STAGES[stage])
        def _():
            outs = [
                Keeper(
                    m,
                    (stash.at[i], stash_kept.at[i], sems.at[i]),
                    boxes[min(i, len(boxes) - 1)],
                    slot=slots[layer],
                    layer=layer,
                    hats=hats,
                    kept=kept,
                )
                for i, layer in enumerate(layers)
            ]
            for i, out in enumerate(outs):
                source = moved if i == 0 else sent
                sent[...] = forward(source[...], *weights[i], out)
            for out in outs:
                out.wait()

    def forward_stage(stage, slots, boxes, weights):
        nonlocal hats, kept
        for m in range(MICROS):
            *boxes, hats, kept, sent = call(
                functools.partial(forward_kernel, stage, slots, m),
                "forward_%d_%d" % (stage, m),
                in_vmem(moved[m], *[a for layer in slots for a in weights[layer]]),
                places=(*boxes, hats, kept),
                new=(block,),
                scratch=keeping(len(slots)),
            )
            moved[m] = send_on(sent, stage)
        return boxes

    weights = fresh_weights("load_1", lambda fold: fold == 1, (0,), 1, 0)
    (box_early,) = forward_stage(1, {0: 0}, [box_early], weights)

    def none(name, array):
        return new_boxes(name, [array.shape])[0]

    box_early, kept = lax.optimization_barrier((box_early, kept))
    got_early = lax.cond(fold_here <= 1, exchange, functools.partial(none, "none_early"), box_early)
    got_early, box_two, kept, hats, raw_in, raw_out = lax.optimization_barrier(
        (got_early, box_two, kept, hats, raw_in, raw_out)
    )
    weights = fresh_weights("load_2", lambda fold: fold == 2, (0,), 1, 0)
    (box_two,) = forward_stage(2, {0: 0}, [box_two], weights)
    raw_in, raw_out, kept = lax.optimization_barrier((raw_in, raw_out, kept))
    weights = fresh_weights("load_3", lambda fold: fold == 3, (0, 1), 1, 0)
    box_two, box_late_two = forward_stage(3, {0: 0, 1: 2}, [box_two, box_late_two], weights)
    raw_in, raw_out, kept = lax.optimization_barrier((raw_in, raw_out, kept))
    weights = fresh_weights("load_4", lambda fold: fold == 2, (1,), 1, 0)
    (box_late_two,) = forward_stage(4, {1: 2}, [box_late_two], [None, *weights])

    box_two, kept = lax.optimization_barrier((box_two, kept))
    got_two = lax.cond(fold_here >= 2, exchange, functools.partial(none, "none_two"), box_two)
    got_two, box_near, box_one, kept, hats, raw_in, raw_out = lax.optimization_barrier(
        (got_two, box_near, box_one, kept, hats, raw_in, raw_out)
    )
    (near,) = fresh_weights("load_near", lambda fold: fold <= 1, (1,), 1, 1)
    (box_one,) = forward_stage(5, {1: 0}, [box_one], [None, near[:3]])

    def middle_kernel(m, reads, box, kept, sent, staged, sem, stash, stash_kept, sems):
        moved, cotangent, gain, weight_in, weight_in_t, weight_out_t = reads
        fold, half = place()

        @pl.when(fold == STAGES[6])
        def _():
            copy = pltpu.make_async_copy(cotangent.at[half, of_micro(m)], staged, sem)
            copy.start()
            outs = [
                Keeper(m, (stash.at[i], stash_kept.at[0], sems.at[i]), box, slot=i)
                for i in range(2)
            ]
            forward(moved[...], gain, weight_in, None, outs[0])
            copy.wait()
            sent[...] = backward(
                staged[...], gain, weight_in_t, weight_out_t, outs[1], lambda: stash_kept.at[0],
                lambda chip: stash[0, chip, :, :chunk],
            )
            for out in outs:
                out.wait()

    for m in range(MICROS):
        box_near, kept, sent = call(
            functools.partial(middle_kernel, m),
            "middle_%d" % m,
            [(moved[m], VMEM), (cotangent, HBM)] + in_vmem(near[0], near[1], near[3], near[4]),
            places=(box_near, kept),
            new=(block,),
            scratch=[block, dma(())] + keeping(2),
        )
        moved[m] = send_on(sent, 6)

    def saved_rows(name, here, layer):
        def kernel(reads, hats_out, kept_out, sems):
            fold, _ = place()
            at = pl.ds(layer * rows, rows)

            @pl.when(here(fold))
            def _():
                copies = [
                    pltpu.make_async_copy(reads[0].at[chip, at, :], hats_out.at[chip], sems.at[chip])
                    for chip in range(chips)
                ]
                copies.append(pltpu.make_async_copy(reads[1].at[at, :], kept_out, sems.at[chips]))
                for copy in copies:
                    copy.start()
                wait_all(copies)

        return call(
            kernel,
            name,
            [(in_hbm(hats), HBM), (in_hbm(kept), HBM)],
            new=(pltpu.VMEM((chips, rows, chunk), bf16), pltpu.VMEM((rows, branch + 128), f32)),
            scratch=[dma((chips + 1,))],
        )

    def backward_kernel(stage, slots, m, reads, box, kept, *refs):
        moved = reads[0]
        layers = list(slots)
        weights = [reads[1 + 5 * i : 4 + 5 * i] for i in range(len(layers))]
        saved = [reads[4 + 5 * i : 6 + 5 * i] for i in range(len(layers))]
        sent = refs[0] if stage < LAST else None
        stash, stash_kept, sems = refs[-3:]
        fold, _ = place()

        @pl.when(fold == STAGES[stage])
        def _():
            outs = [
                Keeper(m, (stash.at[i], stash_kept.at[i], sems.at[i]), box, slot=slots[layer])
                for i, layer in enumerate(layers)
            ]
            for i, out in enumerate(outs):
                source = moved if i == 0 else sent
                have_hats, have = saved[i]
                result = backward(
                    source[...], *weights[i], out, lambda have=have: have.at[of_micro(m)],
                    (lambda chip, hats=have_hats: hats[chip, of_micro(m), :])
                    if sent is not None
                    else None,
                )
                if sent is not None:
                    sent[...] = result
            for out in outs:
                out.wait()

    def backward_stage(stage, slots, box, weights):
        nonlocal kept
        n = len(slots)
        for m in range(MICROS):
            box, kept, *sent = call(
                functools.partial(backward_kernel, stage, slots, m),
                "backward_%d_%d" % (stage, m),
                in_vmem(moved[m], *[a for layer in slots for a in weights[layer]]) ,
                places=(box, kept),
                new=(block,) if stage < LAST else (),
                scratch=keeping(n),
            )
            if sent:
                moved[m] = send_on(sent[0], stage)
        return box

    saved_2 = saved_rows("saved_near_2", lambda fold: fold == 1, 1)
    box_late = backward_stage(7, {1: 0}, box_late, [None, (near[0], *near[3:], *saved_2)])

    box_near, box_one, kept = lax.optimization_barrier((box_near, box_one, kept))
    got_near, got_one = lax.switch(
        jnp.minimum(fold_here, 2),
        (
            lambda near, one: (exchange(near), none("none_one", one)),
            lambda near, one: (none("none_near", near), exchange(one)),
            lambda near, one: (none("none_near", near), none("none_one", one)),
        ),
        box_near,
        box_one,
    )
    got_near, got_one, box_late, box_late_two, box_end, kept, raw_in, raw_out = lax.optimization_barrier(
        (got_near, got_one, box_late, box_late_two, box_end, kept, raw_in, raw_out)
    )
    (far_2,) = fresh_weights("turn_far_2", lambda fold: fold >= 2, (1,), 0, 1)
    far_2 = (*far_2, *saved_rows("saved_far_2", lambda fold: fold >= 2, 1))
    box_late_two = backward_stage(8, {1: 0}, box_late_two, [None, far_2])
    kept, raw_in, raw_out = lax.optimization_barrier((kept, raw_in, raw_out))
    (far_1,) = fresh_weights("turn_far_1", lambda fold: fold >= 2, (0,), 0, 1)
    far_1 = (*far_1, *saved_rows("saved_far_1", lambda fold: fold >= 2, 0))
    box_late_two = backward_stage(9, {1: 0, 0: 1}, box_late_two, [far_1, far_2])
    box_late_two = backward_stage(10, {0: 1}, box_late_two, [far_1])
    kept, raw_in, raw_out = lax.optimization_barrier((kept, raw_in, raw_out))
    (near_1,) = fresh_weights("turn_11", lambda fold: fold == 1, (0,), 0, 1)
    near_1 = (*near_1, *saved_rows("saved_11", lambda fold: fold == 1, 0))
    box_late = backward_stage(11, {0: 1}, box_late, [near_1])

    box_late, box_late_two, kept = lax.optimization_barrier((box_late, box_late_two, kept))
    got_late, got_late_two = lax.switch(
        jnp.minimum(fold_here, 2),
        (
            lambda late, late_two: (none("none_late", late), none("none_late_two", late_two)),
            lambda late, late_two: (exchange(late, raw=True), none("none_late_two", late_two)),
            lambda late, late_two: (none("none_late", late), exchange(late_two, raw=True)),
        ),
        box_late,
        box_late_two,
    )
    got_late, got_late_two, box_end, kept, raw_in, raw_out = lax.optimization_barrier(
        (got_late, got_late_two, box_end, kept, raw_in, raw_out)
    )
    (near_1,) = fresh_weights("turn_12", lambda fold: fold == 0, (0,), 0, 1)
    near_1 = (*near_1, *saved_rows("saved_12", lambda fold: fold == 0, 0))
    box_end = backward_stage(LAST, {0: 0}, box_end, [near_1])

    def products(pick, reads, keep, send, whole_in, whole_out):
        _, half = place()
        core = lax.rem(lax.axis_index("dp"), 2)
        mine = pl.ds(pl.multiple_of(core * branch, branch), branch)
        theirs = pl.ds(pl.multiple_of((1 - core) * branch, branch), branch)
        narrow, wide = slice(chunk, pack), slice(0, chunk)

        def part(which, columns):
            box, slot = which
            return reads[box][:, slot * rows : (slot + 1) * rows, columns].reshape(chips * rows, -1)

        for layer, slot in ((0, half), (1, 1 - half)):
            hat, up = pick[layer]
            whole_in[...] = transposed_matmul(part(hat, wide), part(up, narrow))
            whole_out[...] = transposed_matmul(part(hat, narrow), part(up, wide))
            keep[slot, 0] = whole_in[mine, :]
            keep[slot, 1] = whole_out[:, mine]
            send[slot, 0] = whole_in[theirs, :].astype(bf16)
            send[slot, 1] = whole_out[:, theirs].astype(bf16)

    def finish(name, pick, *boxes):
        return call(
            functools.partial(products, pick),
            name,
            in_vmem(*boxes),
            new=(pltpu.VMEM((2, 2, branch, branch), f32), pltpu.VMEM((2, 2, branch, branch), bf16)),
            scratch=[pltpu.VMEM((2 * branch, branch), f32), pltpu.VMEM((branch, 2 * branch), f32)],
        )

    near_pick = (((0, 0), (1, 1)), ((2, 0), (1, 0)))
    far_pick = (((0, 0), (1, 1)), ((1, 2), (1, 0)))
    keep, send = lax.switch(
        jnp.minimum(fold_here, 2),
        (
            lambda end, late, late_two, early, near, one, two: finish(
                "products_0", (((0, 0), (1, 0)), ((2, 0), (2, 1))), early, exchange(end, raw=True), near
            ),
            lambda end, late, late_two, early, near, one, two: finish(
                "products_1", near_pick, early, late, one
            ),
            lambda end, late, late_two, early, near, one, two: finish(
                "products_2", far_pick, two, late_two
            ),
        ),
        box_end,
        got_late,
        got_late_two,
        got_early,
        got_near,
        got_one,
        got_two,
    )
    total = keep + lax.ppermute(send, "dp", [(i, i ^ 1) for i in range(parts)]).astype(f32)
    mirror = [(s, sections - 1 - s) for s in range(sections)]
    total = total[0] + lax.ppermute(total[1].astype(bf16), "section", mirror).astype(f32)
    start = lax.axis_index("dp") * branch
    own_gain = lax.dynamic_slice_in_dim(gain[0], start, branch, 0)
    own_in = lax.dynamic_slice_in_dim(raw_in[0], start, branch, 0).astype(f32)
    grad_in = total[0] * own_gain[:, None]
    grad_gain = jnp.sum(total[0] * own_in, axis=1)
    return (grad_in[None], total[1][None], grad_gain[None])


def solution(mesh):
    return jax.shard_map(
        on_device,
        mesh=mesh,
        in_specs=(
            P(None, "dp", None),
            P(None, "dp", None),
            P("section", None, None),
            P("section", None, None),
            P("section", None),
        ),
        out_specs=(P("section", "dp", None), P("section", None, "dp"), P("section", "dp")),
        check_vma=False,
    )
```

```python
import functools

import jax
import jax.numpy as jnp
from jax import lax
from jax.experimental import pallas as pl
from jax.experimental.pallas import tpu as pltpu
from jax.sharding import PartitionSpec as P

epsilon = 1e-05
STAGES = (0, 1, 2, 3, 2, 1, 0, 1, 2, 3, 2, 1, 0)
LAST = len(STAGES) - 1
MICROS = 2
bf16 = jnp.bfloat16
f32 = jnp.float32
VMEM = pl.BlockSpec(memory_space=pltpu.VMEM)
HBM = pl.BlockSpec(memory_space=pltpu.HBM)
LOADS = 8
MIB = 2**20


def matmul(left, right):
    return jnp.dot(left, right, preferred_element_type=f32)


def transposed_matmul(left, right):
    return lax.dot_general(left, right, (((0,), (0,)), ((), ())), preferred_element_type=f32)


def place():
    sections = lax.axis_size("section")
    position = lax.axis_index("section")
    half = (position >= sections // 2).astype(jnp.int32)
    fold = jnp.where(half == 0, position, sections - 1 - position)
    return fold, half


def call(body, name, reads, updates=(), places=(), new=(), scratch=(), limit=16):
    n_read, n_update, n_place = len(reads), len(updates), len(places)

    def kernel(*refs):
        ins, outs = refs[: n_read + n_update + n_place], refs[n_read + n_update + n_place :]
        for old, now in zip(ins[n_read : n_read + n_update], outs):
            now[...] = old[...]
        body(ins[:n_read], *outs)

    shapes = [pltpu.VMEM(a.shape, a.dtype) for a in updates]
    shapes += [pltpu.HBM(a.shape, a.dtype) for a in places]
    shapes += list(new)
    kept = [VMEM] * n_update + [HBM] * n_place
    return pl.pallas_call(
        kernel,
        out_shape=tuple(shapes),
        in_specs=[spec for _, spec in reads] + kept,
        out_specs=tuple(kept + [VMEM] * len(new)),
        input_output_aliases={n_read + i: i for i in range(n_update + n_place)},
        scratch_shapes=list(scratch),
        compiler_params=pltpu.CompilerParams(vmem_limit_bytes=limit * MIB),
        cost_estimate=pl.CostEstimate(flops=1, bytes_accessed=1, transcendentals=0),
        name=name,
    )(*[a for a, _ in reads], *updates, *places)


def load(copy, sources, targets, sems):
    waits = []
    for which, (source, target) in enumerate(zip(sources, targets)):
        size = source.shape[1] // LOADS
        pieces = []
        for i in range(LOADS):
            part = pl.ds(i * size, size)
            pieces.append(
                pltpu.make_async_copy(
                    source.at[copy, part], target.at[part], sems.at[which * LOADS + i]
                )
            )
        for piece in pieces:
            piece.start()
        waits.append(pieces)
    return waits


def wait_all(pieces):
    for piece in pieces:
        piece.wait()


def forward(source, gain, weight_in, weight_out, out, ready=None):
    chips = out.rows.shape[0]
    micro, width = source.shape
    branch = weight_in.shape[1]
    chunk = width // chips
    wide = source.astype(f32)
    scaling = lax.rsqrt(jnp.mean(wide * wide, axis=-1, keepdims=True) + epsilon)
    normal = wide * scaling
    if ready is not None:
        wait_all(ready[0])
    before = matmul((normal * gain[...]).astype(bf16), weight_in[...])
    inner = (before * jax.nn.sigmoid(before)).astype(bf16)
    out.kept[:, :branch] = before
    out.kept[:, branch:] = jnp.broadcast_to(scaling, (micro, 128))
    for chip in range(chips):
        out.rows[chip, :, :chunk] = normal[:, chip * chunk : (chip + 1) * chunk].astype(bf16)
        out.rows[chip, :, chunk:] = inner
    out.start()
    if ready is not None:
        wait_all(ready[1])
    if weight_out is not None:
        return (wide + matmul(inner, weight_out[...])).astype(bf16)


def backward(grad, gain, weight_in_t, weight_out_t, out, saved, hats):
    chips = out.rows.shape[0]
    width = grad.shape[1]
    branch = weight_in_t.shape[0]
    chunk = width // chips
    d_inner = matmul(grad, weight_out_t[...])
    kept = saved()
    before = kept[:, :branch]
    sigma = jax.nn.sigmoid(before)
    delta = (d_inner * sigma * (1.0 + before * (1.0 - sigma))).astype(bf16)
    for chip in range(chips):
        out.rows[chip, :, :chunk] = grad[:, chip * chunk : (chip + 1) * chunk]
        out.rows[chip, :, chunk:] = delta
    out.start()
    if hats is None:
        return None
    mixed = jnp.sum(delta.astype(f32) * before, axis=-1, keepdims=True) / width
    scaled = matmul(delta, weight_in_t[...]) * gain[...]
    scaling = kept[:, branch : branch + 1]
    result = []
    for chip in range(chips):
        part = slice(chip * chunk, (chip + 1) * chunk)
        normal = hats(chip).astype(f32)
        result.append(
            (grad[:, part].astype(f32) + scaling * (scaled[:, part] - normal * mixed)).astype(bf16)
        )
    return jnp.concatenate(result, axis=1)


def on_device(inputs, cotangent, w_in, w_out, gain):
    sections = lax.axis_size("section")
    parts = lax.axis_size("dp")
    chips = parts // 2
    rows, width = inputs.shape[1:]
    micro = rows // MICROS
    branch = w_in.shape[2]
    chunk = width // chips
    pack = chunk + branch

    def in_hbm(array):
        return pltpu.with_memory_space_constraint(array, pltpu.HBM)

    raw_in, raw_out = w_in, w_out
    inputs, cotangent, w_in, w_out = map(in_hbm, (inputs, cotangent, w_in, w_out))
    dma = pltpu.SemaphoreType.DMA
    block = pltpu.VMEM((micro, width), bf16)
    packed = pltpu.VMEM((chips, micro, pack), bf16)
    in_shape, out_shape = pltpu.VMEM((width, branch), bf16), pltpu.VMEM((branch, width), bf16)
    in_turned, out_turned = out_shape, in_shape
    row_shape = pltpu.VMEM((1, width), f32)
    load_sems = dma((2 * LOADS,))
    fold_here, _ = place()
    same_core = [list(range(core, parts, 2)) for core in range(2)]

    def of_micro(m):
        return pl.ds(m * micro, micro)

    def send_on(sent, stage):
        a, b = STAGES[stage], STAGES[stage + 1]
        pairs = [(a, b), (sections - 1 - a, sections - 1 - b)]
        return lax.ppermute(sent, "section", pairs)

    def copy_kernel(reads, target, sems):
        copies = [
            pltpu.make_async_copy(reads[0].at[chip], target.at[chip], sems.at[chip])
            for chip in range(chips)
        ]
        for copy in copies:
            copy.start()
        wait_all(copies)

    def exchange(array, raw=False):
        array = lax.all_to_all(array, "dp", 0, 0, axis_index_groups=same_core, tiled=False)
        if raw:
            return array
        array = pltpu.with_memory_space_constraint(array, pltpu.VMEM)
        (target,) = new_boxes("unstage_box", [array.shape])
        (target,) = call(copy_kernel, "unstage", [(array, VMEM)], places=(target,), scratch=[dma((chips,))])
        return target

    def new_boxes(name, shapes):
        shapes = [pltpu.HBM(shape, bf16) for shape in shapes]
        return pl.pallas_call(
            lambda *refs: None, out_shape=tuple(shapes), out_specs=(HBM,) * len(shapes), name=name
        )()

    def in_vmem(*arrays):
        return [(a, VMEM) for a in arrays]

    (box_early,) = new_boxes("box_early", [(chips, rows, pack)])
    (box_two,) = new_boxes("box_two", [(chips, rows, pack)])
    box_near, box_one = new_boxes("box_near", [(chips, 2 * rows, pack), (chips, rows, pack)])
    box_late, box_late_two, box_end = new_boxes(
        "box_late", [(chips, n * rows, pack) for n in (2, 3, 1)]
    )
    (hats,) = new_boxes("hats", [(chips, 2 * rows, chunk)])

    def start_kernel(reads, box, kept, sent, gain, weight_in, weight_out, staged, sem, load_sems, *scratch):
        inputs, source_in, source_out, source_gain = reads
        fold, half = place()

        @pl.when(fold == STAGES[0])
        def _():
            copy = pltpu.make_async_copy(inputs.at[half, of_micro(0)], staged, sem)
            copy.start()
            ready = load(half, (source_in, source_out), (weight_in, weight_out), load_sems)
            gain[...] = source_gain[pl.ds(half, 1), :]
            copy.wait()
            out = Keeper(0, scratch, box, layer=0, kept=kept)
            sent[...] = forward(staged[...], gain, weight_in, weight_out, out, ready)
            out.wait()

    class Keeper:
        def __init__(self, m, scratch, box, slot=0, layer=0, hats=None, kept=None):
            self.rows, self.kept, sems = scratch
            own = pl.ds(layer * rows + m * micro, micro)
            at = pl.ds(slot * rows + m * micro, micro)
            pairs = [(self.rows, box.at[:, at, :])]
            if hats is not None:
                pairs.append((self.rows.at[:, :, pl.ds(0, chunk)], hats.at[:, own, :]))
            if kept is not None:
                pairs.append((self.kept, kept.at[own, :]))
            self.copies = [
                pltpu.make_async_copy(source, target, sems.at[i])
                for i, (source, target) in enumerate(pairs)
            ]

        def start(self):
            for copy in self.copies:
                copy.start()

        def wait(self):
            wait_all(self.copies)

    kept_shape = pltpu.HBM((2 * rows, branch + 128), f32)
    kept_block = pltpu.VMEM((micro, branch + 128), f32)
    (kept,) = pl.pallas_call(
        lambda *refs: None, out_shape=(kept_shape,), out_specs=(HBM,), name="kept"
    )()

    copies = 3

    def keeping(n=1):
        return [
            pltpu.VMEM((n, chips, micro, pack), bf16),
            pltpu.VMEM((n, micro, branch + 128), f32),
            dma((n, copies)),
        ]

    keeping_one = [packed, kept_block, dma((copies,))]
    moved = [None] * MICROS
    box_early, kept, sent, *weights_1 = call(
        start_kernel,
        "forward_0_0",
        [(inputs, HBM), (w_in, HBM), (w_out, HBM), (gain, VMEM)],
        places=(box_early, kept),
        new=(block, row_shape, in_shape, out_shape),
        scratch=[block, dma(()), load_sems] + keeping_one,
    )
    moved[0] = send_on(sent, 0)
    for m in range(1, MICROS):

        def input_kernel(reads, box, kept, sent, staged, sem, *scratch, m=m):
            inputs, *weights = reads
            fold, half = place()

            @pl.when(fold == STAGES[0])
            def _():
                copy = pltpu.make_async_copy(inputs.at[half, of_micro(m)], staged, sem)
                copy.start()
                copy.wait()
                out = Keeper(m, scratch, box, layer=0, kept=kept)
                sent[...] = forward(staged[...], *weights, out)
                out.wait()

        box_early, kept, sent = call(
            input_kernel,
            "forward_0_%d" % m,
            [(inputs, HBM)] + in_vmem(*weights_1),
            places=(box_early, kept),
            new=(block,),
            scratch=[block, dma(())] + keeping_one,
        )
        moved[m] = send_on(sent, 0)

    def turn(weight_in, weight_out, weight_in_t, weight_out_t):
        @pl.loop(0, width // branch)
        def _(tile):
            part = pl.ds(pl.multiple_of(tile * branch, branch), branch)
            weight_in_t[:, part] = weight_in[part, :].T
            weight_out_t[part, :] = weight_out[:, part].T

    def fresh_weights(name, here, layers, plain, turned):
        def kernel(reads, *refs):
            source_in, source_out, source_gain = reads
            fold, half = place()
            sems, raw = refs[-1], refs[-3:-1]

            @pl.when(here(fold))
            def _():
                waits, at = [], 0
                for i, layer in enumerate(layers):
                    copy = half if layer == 0 else 1 - half
                    gain, *targets = refs[at : at + 1 + 2 * (plain + turned)]
                    at += 1 + 2 * (plain + turned)
                    gain[...] = source_gain[pl.ds(copy, 1), :]
                    loaded = targets[:2] if plain else raw
                    waits.append(load(copy, (source_in, source_out), loaded, sems.at[i]))
                    if turned:
                        wait_all(waits[i][0] + waits[i][1])
                        turn(*loaded, *targets[-2:])
                if not turned:
                    for wait in waits:
                        wait_all(wait[0] + wait[1])

        shapes = (row_shape,) + (in_shape, out_shape) * plain + (in_turned, out_turned) * turned
        outs = call(
            kernel,
            name,
            [(in_hbm(raw_in), HBM), (in_hbm(raw_out), HBM), (gain, VMEM)],
            new=shapes * len(layers),
            scratch=[in_shape, out_shape, dma((len(layers), 2 * LOADS))],
        )
        return [outs[i * len(shapes) : (i + 1) * len(shapes)] for i in range(len(layers))]

    def forward_kernel(stage, slots, m, reads, *refs):
        moved = reads[0]
        boxes, (hats, kept, sent, stash, stash_kept, sems) = refs[:-6], refs[-6:]
        layers = list(slots)
        weights = [reads[1 + 3 * i : 4 + 3 * i] for i in range(len(layers))]
        fold, _ = place()

        @pl.when(fold == STAGES[stage])
        def _():
            outs = [
                Keeper(
                    m,
                    (stash.at[i], stash_kept.at[i], sems.at[i]),
                    boxes[min(i, len(boxes) - 1)],
                    slot=slots[layer],
                    layer=layer,
                    hats=hats,
                    kept=kept,
                )
                for i, layer in enumerate(layers)
            ]
            for i, out in enumerate(outs):
                source = moved if i == 0 else sent
                sent[...] = forward(source[...], *weights[i], out)
            for out in outs:
                out.wait()

    def forward_stage(stage, slots, boxes, weights):
        nonlocal hats, kept
        for m in range(MICROS):
            *boxes, hats, kept, sent = call(
                functools.partial(forward_kernel, stage, slots, m),
                "forward_%d_%d" % (stage, m),
                in_vmem(moved[m], *[a for layer in slots for a in weights[layer]]),
                places=(*boxes, hats, kept),
                new=(block,),
                scratch=keeping(len(slots)),
            )
            moved[m] = send_on(sent, stage)
        return boxes

    weights = fresh_weights("load_1", lambda fold: fold == 1, (0,), 1, 0)
    (box_early,) = forward_stage(1, {0: 0}, [box_early], weights)

    def none(name, array):
        return new_boxes(name, [array.shape])[0]

    box_early, kept = lax.optimization_barrier((box_early, kept))
    got_early = lax.cond(fold_here <= 1, exchange, functools.partial(none, "none_early"), box_early)
    got_early, box_two, kept, hats, raw_in, raw_out = lax.optimization_barrier(
        (got_early, box_two, kept, hats, raw_in, raw_out)
    )
    weights = fresh_weights("load_2", lambda fold: fold == 2, (0,), 1, 0)
    (box_two,) = forward_stage(2, {0: 0}, [box_two], weights)
    raw_in, raw_out, kept = lax.optimization_barrier((raw_in, raw_out, kept))
    weights = fresh_weights("load_3", lambda fold: fold == 3, (0, 1), 1, 0)
    box_two, box_late_two = forward_stage(3, {0: 0, 1: 2}, [box_two, box_late_two], weights)
    raw_in, raw_out, kept = lax.optimization_barrier((raw_in, raw_out, kept))
    weights = fresh_weights("load_4", lambda fold: fold == 2, (1,), 1, 0)
    (box_late_two,) = forward_stage(4, {1: 2}, [box_late_two], [None, *weights])

    box_two, kept = lax.optimization_barrier((box_two, kept))
    got_two = lax.cond(fold_here >= 2, exchange, functools.partial(none, "none_two"), box_two)
    got_two, box_near, box_one, kept, hats, raw_in, raw_out = lax.optimization_barrier(
        (got_two, box_near, box_one, kept, hats, raw_in, raw_out)
    )
    (near,) = fresh_weights("load_near", lambda fold: fold <= 1, (1,), 1, 1)
    (box_one,) = forward_stage(5, {1: 0}, [box_one], [None, near[:3]])

    def middle_kernel(m, reads, box, kept, sent, staged, sem, stash, stash_kept, sems):
        moved, cotangent, gain, weight_in, weight_in_t, weight_out_t = reads
        fold, half = place()

        @pl.when(fold == STAGES[6])
        def _():
            copy = pltpu.make_async_copy(cotangent.at[half, of_micro(m)], staged, sem)
            copy.start()
            outs = [
                Keeper(m, (stash.at[i], stash_kept.at[0], sems.at[i]), box, slot=i)
                for i in range(2)
            ]
            forward(moved[...], gain, weight_in, None, outs[0])
            copy.wait()
            sent[...] = backward(
                staged[...], gain, weight_in_t, weight_out_t, outs[1], lambda: stash_kept.at[0],
                lambda chip: stash[0, chip, :, :chunk],
            )
            for out in outs:
                out.wait()

    for m in range(MICROS):
        box_near, kept, sent = call(
            functools.partial(middle_kernel, m),
            "middle_%d" % m,
            [(moved[m], VMEM), (cotangent, HBM)] + in_vmem(near[0], near[1], near[3], near[4]),
            places=(box_near, kept),
            new=(block,),
            scratch=[block, dma(())] + keeping(2),
        )
        moved[m] = send_on(sent, 6)

    def saved_rows(name, here, layer):
        def kernel(reads, hats_out, kept_out, sems):
            fold, _ = place()
            at = pl.ds(layer * rows, rows)

            @pl.when(here(fold))
            def _():
                copies = [
                    pltpu.make_async_copy(reads[0].at[chip, at, :], hats_out.at[chip], sems.at[chip])
                    for chip in range(chips)
                ]
                copies.append(pltpu.make_async_copy(reads[1].at[at, :], kept_out, sems.at[chips]))
                for copy in copies:
                    copy.start()
                wait_all(copies)

        return call(
            kernel,
            name,
            [(in_hbm(hats), HBM), (in_hbm(kept), HBM)],
            new=(pltpu.VMEM((chips, rows, chunk), bf16), pltpu.VMEM((rows, branch + 128), f32)),
            scratch=[dma((chips + 1,))],
        )

    def backward_kernel(stage, slots, m, reads, box, kept, *refs):
        moved = reads[0]
        layers = list(slots)
        weights = [reads[1 + 5 * i : 4 + 5 * i] for i in range(len(layers))]
        saved = [reads[4 + 5 * i : 6 + 5 * i] for i in range(len(layers))]
        sent = refs[0] if stage < LAST else None
        stash, stash_kept, sems = refs[-3:]
        fold, _ = place()

        @pl.when(fold == STAGES[stage])
        def _():
            outs = [
                Keeper(m, (stash.at[i], stash_kept.at[i], sems.at[i]), box, slot=slots[layer])
                for i, layer in enumerate(layers)
            ]
            for i, out in enumerate(outs):
                source = moved if i == 0 else sent
                have_hats, have = saved[i]
                result = backward(
                    source[...], *weights[i], out, lambda have=have: have.at[of_micro(m)],
                    (lambda chip, hats=have_hats: hats[chip, of_micro(m), :])
                    if sent is not None
                    else None,
                )
                if sent is not None:
                    sent[...] = result
            for out in outs:
                out.wait()

    def backward_stage(stage, slots, box, weights):
        nonlocal kept
        n = len(slots)
        for m in range(MICROS):
            box, kept, *sent = call(
                functools.partial(backward_kernel, stage, slots, m),
                "backward_%d_%d" % (stage, m),
                in_vmem(moved[m], *[a for layer in slots for a in weights[layer]]) ,
                places=(box, kept),
                new=(block,) if stage < LAST else (),
                scratch=keeping(n),
            )
            if sent:
                moved[m] = send_on(sent[0], stage)
        return box

    saved_2 = saved_rows("saved_near_2", lambda fold: fold == 1, 1)
    box_late = backward_stage(7, {1: 0}, box_late, [None, (near[0], *near[3:], *saved_2)])

    box_near, box_one, kept = lax.optimization_barrier((box_near, box_one, kept))
    got_near, got_one = lax.switch(
        jnp.minimum(fold_here, 2),
        (
            lambda near, one: (exchange(near), none("none_one", one)),
            lambda near, one: (none("none_near", near), exchange(one)),
            lambda near, one: (none("none_near", near), none("none_one", one)),
        ),
        box_near,
        box_one,
    )
    got_near, got_one, box_late, box_late_two, box_end, kept, raw_in, raw_out = lax.optimization_barrier(
        (got_near, got_one, box_late, box_late_two, box_end, kept, raw_in, raw_out)
    )
    (far_2,) = fresh_weights("turn_far_2", lambda fold: fold >= 2, (1,), 0, 1)
    far_2 = (*far_2, *saved_rows("saved_far_2", lambda fold: fold >= 2, 1))
    box_late_two = backward_stage(8, {1: 0}, box_late_two, [None, far_2])
    kept, raw_in, raw_out = lax.optimization_barrier((kept, raw_in, raw_out))
    (far_1,) = fresh_weights("turn_9", lambda fold: fold == 3, (0,), 0, 1)
    far_1 = (*far_1, *saved_rows("saved_9", lambda fold: fold == 3, 0))
    box_late_two = backward_stage(9, {1: 0, 0: 1}, box_late_two, [far_1, far_2])
    kept, raw_in, raw_out = lax.optimization_barrier((kept, raw_in, raw_out))
    (far_1,) = fresh_weights("turn_10", lambda fold: fold == 2, (0,), 0, 1)
    far_1 = (*far_1, *saved_rows("saved_10", lambda fold: fold == 2, 0))
    box_late_two = backward_stage(10, {0: 1}, box_late_two, [far_1])

    box_late_two, kept = lax.optimization_barrier((box_late_two, kept))
    got_late_two = lax.cond(
        fold_here >= 2,
        functools.partial(exchange, raw=True),
        functools.partial(none, "none_late_two"),
        box_late_two,
    )
    got_late_two, box_late, kept, hats, raw_in, raw_out = lax.optimization_barrier(
        (got_late_two, box_late, kept, hats, raw_in, raw_out)
    )
    (near_1,) = fresh_weights("turn_11", lambda fold: fold == 1, (0,), 0, 1)
    near_1 = (*near_1, *saved_rows("saved_11", lambda fold: fold == 1, 0))
    box_late = backward_stage(11, {0: 1}, box_late, [near_1])

    box_late, kept = lax.optimization_barrier((box_late, kept))
    got_late = lax.cond(
        fold_here == 1,
        functools.partial(exchange, raw=True),
        functools.partial(none, "none_late"),
        box_late,
    )
    got_late, box_end, kept, raw_in, raw_out = lax.optimization_barrier(
        (got_late, box_end, kept, raw_in, raw_out)
    )
    (near_1,) = fresh_weights("turn_12", lambda fold: fold == 0, (0,), 0, 1)
    near_1 = (*near_1, *saved_rows("saved_12", lambda fold: fold == 0, 0))
    box_end = backward_stage(LAST, {0: 0}, box_end, [near_1])

    def products(pick, reads, keep, send, whole_in, whole_out):
        _, half = place()
        core = lax.rem(lax.axis_index("dp"), 2)
        mine = pl.ds(pl.multiple_of(core * branch, branch), branch)
        theirs = pl.ds(pl.multiple_of((1 - core) * branch, branch), branch)
        narrow, wide = slice(chunk, pack), slice(0, chunk)

        def part(which, columns):
            box, slot = which
            return reads[box][:, slot * rows : (slot + 1) * rows, columns].reshape(chips * rows, -1)

        for layer, slot in ((0, half), (1, 1 - half)):
            hat, up = pick[layer]
            whole_in[...] = transposed_matmul(part(hat, wide), part(up, narrow))
            whole_out[...] = transposed_matmul(part(hat, narrow), part(up, wide))
            keep[slot, 0] = whole_in[mine, :]
            keep[slot, 1] = whole_out[:, mine]
            send[slot, 0] = whole_in[theirs, :].astype(bf16)
            send[slot, 1] = whole_out[:, theirs].astype(bf16)

    def finish(name, pick, *boxes):
        return call(
            functools.partial(products, pick),
            name,
            in_vmem(*boxes),
            new=(pltpu.VMEM((2, 2, branch, branch), f32), pltpu.VMEM((2, 2, branch, branch), bf16)),
            scratch=[pltpu.VMEM((2 * branch, branch), f32), pltpu.VMEM((branch, 2 * branch), f32)],
        )

    near_pick = (((0, 0), (1, 1)), ((2, 0), (1, 0)))
    far_pick = (((0, 0), (1, 1)), ((1, 2), (1, 0)))
    keep, send = lax.switch(
        jnp.minimum(fold_here, 2),
        (
            lambda end, late, late_two, early, near, one, two: finish(
                "products_0", (((0, 0), (1, 0)), ((2, 0), (2, 1))), early, exchange(end, raw=True), near
            ),
            lambda end, late, late_two, early, near, one, two: finish(
                "products_1", near_pick, early, late, one
            ),
            lambda end, late, late_two, early, near, one, two: finish(
                "products_2", far_pick, two, late_two
            ),
        ),
        box_end,
        got_late,
        got_late_two,
        got_early,
        got_near,
        got_one,
        got_two,
    )
    total = keep + lax.ppermute(send, "dp", [(i, i ^ 1) for i in range(parts)]).astype(f32)
    mirror = [(s, sections - 1 - s) for s in range(sections)]
    total = total[0] + lax.ppermute(total[1].astype(bf16), "section", mirror).astype(f32)
    start = lax.axis_index("dp") * branch
    own_gain = lax.dynamic_slice_in_dim(gain[0], start, branch, 0)
    own_in = lax.dynamic_slice_in_dim(raw_in[0], start, branch, 0).astype(f32)
    grad_in = total[0] * own_gain[:, None]
    grad_gain = jnp.sum(total[0] * own_in, axis=1)
    return (grad_in[None], total[1][None], grad_gain[None])


def solution(mesh):
    return jax.shard_map(
        on_device,
        mesh=mesh,
        in_specs=(
            P(None, "dp", None),
            P(None, "dp", None),
            P("section", None, None),
            P("section", None, None),
            P("section", None),
        ),
        out_specs=(P("section", "dp", None), P("section", None, "dp"), P("section", "dp")),
        check_vma=False,
    )
```

```python
import functools

import jax
import jax.numpy as jnp
from jax import lax
from jax.experimental import pallas as pl
from jax.experimental.pallas import tpu as pltpu
from jax.sharding import PartitionSpec as P

epsilon = 1e-05
STAGES = (0, 1, 2, 3, 2, 1, 0, 1, 2, 3, 2, 1, 0)
LAST = len(STAGES) - 1
MICROS = 2
bf16 = jnp.bfloat16
f32 = jnp.float32
VMEM = pl.BlockSpec(memory_space=pltpu.VMEM)
HBM = pl.BlockSpec(memory_space=pltpu.HBM)
LOADS = 8
MIB = 2**20


def matmul(left, right):
    return jnp.dot(left, right, preferred_element_type=f32)


def transposed_matmul(left, right):
    return lax.dot_general(left, right, (((0,), (0,)), ((), ())), preferred_element_type=f32)


def place():
    sections = lax.axis_size("section")
    position = lax.axis_index("section")
    half = (position >= sections // 2).astype(jnp.int32)
    fold = jnp.where(half == 0, position, sections - 1 - position)
    return fold, half


def call(body, name, reads, updates=(), places=(), new=(), scratch=(), limit=16):
    n_read, n_update, n_place = len(reads), len(updates), len(places)

    def kernel(*refs):
        ins, outs = refs[: n_read + n_update + n_place], refs[n_read + n_update + n_place :]
        for old, now in zip(ins[n_read : n_read + n_update], outs):
            now[...] = old[...]
        body(ins[:n_read], *outs)

    shapes = [pltpu.VMEM(a.shape, a.dtype) for a in updates]
    shapes += [pltpu.HBM(a.shape, a.dtype) for a in places]
    shapes += list(new)
    kept = [VMEM] * n_update + [HBM] * n_place
    return pl.pallas_call(
        kernel,
        out_shape=tuple(shapes),
        in_specs=[spec for _, spec in reads] + kept,
        out_specs=tuple(kept + [VMEM] * len(new)),
        input_output_aliases={n_read + i: i for i in range(n_update + n_place)},
        scratch_shapes=list(scratch),
        compiler_params=pltpu.CompilerParams(vmem_limit_bytes=limit * MIB),
        cost_estimate=pl.CostEstimate(flops=1, bytes_accessed=1, transcendentals=0),
        name=name,
    )(*[a for a, _ in reads], *updates, *places)


def load(copy, sources, targets, sems):
    waits = []
    for which, (source, target) in enumerate(zip(sources, targets)):
        size = source.shape[1] // LOADS
        pieces = []
        for i in range(LOADS):
            part = pl.ds(i * size, size)
            pieces.append(
                pltpu.make_async_copy(
                    source.at[copy, part], target.at[part], sems.at[which * LOADS + i]
                )
            )
        for piece in pieces:
            piece.start()
        waits.append(pieces)
    return waits


def wait_all(pieces):
    for piece in pieces:
        piece.wait()


def forward(source, gain, weight_in, weight_out, out, ready=None):
    chips = out.rows.shape[0]
    micro, width = source.shape
    branch = weight_in.shape[1]
    chunk = width // chips
    wide = source.astype(f32)
    scaling = lax.rsqrt(jnp.mean(wide * wide, axis=-1, keepdims=True) + epsilon)
    normal = wide * scaling
    if ready is not None:
        wait_all(ready[0])
    before = matmul((normal * gain[...]).astype(bf16), weight_in[...])
    inner = (before * jax.nn.sigmoid(before)).astype(bf16)
    out.kept[:, :branch] = before
    out.kept[:, branch:] = jnp.broadcast_to(scaling, (micro, 128))
    for chip in range(chips):
        out.rows[chip, :, :chunk] = normal[:, chip * chunk : (chip + 1) * chunk].astype(bf16)
        out.rows[chip, :, chunk:] = inner
    out.start()
    if ready is not None:
        wait_all(ready[1])
    if weight_out is not None:
        return (wide + matmul(inner, weight_out[...])).astype(bf16)


def backward(grad, gain, weight_in_t, weight_out_t, out, saved, hats):
    chips = out.rows.shape[0]
    width = grad.shape[1]
    branch = weight_in_t.shape[0]
    chunk = width // chips
    d_inner = matmul(grad, weight_out_t[...])
    kept = saved()
    before = kept[:, :branch]
    sigma = jax.nn.sigmoid(before)
    delta = (d_inner * sigma * (1.0 + before * (1.0 - sigma))).astype(bf16)
    for chip in range(chips):
        out.rows[chip, :, :chunk] = grad[:, chip * chunk : (chip + 1) * chunk]
        out.rows[chip, :, chunk:] = delta
    out.start()
    if hats is None:
        return None
    mixed = jnp.sum(delta.astype(f32) * before, axis=-1, keepdims=True) / width
    scaled = matmul(delta, weight_in_t[...]) * gain[...]
    scaling = kept[:, branch : branch + 1]
    result = []
    for chip in range(chips):
        part = slice(chip * chunk, (chip + 1) * chunk)
        normal = hats(chip).astype(f32)
        result.append(
            (grad[:, part].astype(f32) + scaling * (scaled[:, part] - normal * mixed)).astype(bf16)
        )
    return jnp.concatenate(result, axis=1)


def on_device(inputs, cotangent, w_in, w_out, gain):
    sections = lax.axis_size("section")
    parts = lax.axis_size("dp")
    chips = parts // 2
    rows, width = inputs.shape[1:]
    micro = rows // MICROS
    branch = w_in.shape[2]
    chunk = width // chips
    pack = chunk + branch

    def in_hbm(array):
        return pltpu.with_memory_space_constraint(array, pltpu.HBM)

    raw_in, raw_out = w_in, w_out
    inputs, cotangent, w_in, w_out = map(in_hbm, (inputs, cotangent, w_in, w_out))
    dma = pltpu.SemaphoreType.DMA
    block = pltpu.VMEM((micro, width), bf16)
    packed = pltpu.VMEM((chips, micro, pack), bf16)
    in_shape, out_shape = pltpu.VMEM((width, branch), bf16), pltpu.VMEM((branch, width), bf16)
    in_turned, out_turned = out_shape, in_shape
    row_shape = pltpu.VMEM((1, width), f32)
    load_sems = dma((2 * LOADS,))
    fold_here, _ = place()
    same_core = [list(range(core, parts, 2)) for core in range(2)]

    def of_micro(m):
        return pl.ds(m * micro, micro)

    def send_on(sent, stage):
        a, b = STAGES[stage], STAGES[stage + 1]
        pairs = [(a, b), (sections - 1 - a, sections - 1 - b)]
        return lax.ppermute(sent, "section", pairs)

    def copy_kernel(reads, target, sems):
        copies = [
            pltpu.make_async_copy(reads[0].at[chip], target.at[chip], sems.at[chip])
            for chip in range(chips)
        ]
        for copy in copies:
            copy.start()
        wait_all(copies)

    def exchange(array, raw=False):
        array = lax.all_to_all(array, "dp", 0, 0, axis_index_groups=same_core, tiled=False)
        if raw:
            return array
        array = pltpu.with_memory_space_constraint(array, pltpu.VMEM)
        (target,) = new_boxes("unstage_box", [array.shape])
        (target,) = call(copy_kernel, "unstage", [(array, VMEM)], places=(target,), scratch=[dma((chips,))])
        return target

    def new_boxes(name, shapes):
        shapes = [pltpu.HBM(shape, bf16) for shape in shapes]
        return pl.pallas_call(
            lambda *refs: None, out_shape=tuple(shapes), out_specs=(HBM,) * len(shapes), name=name
        )()

    def in_vmem(*arrays):
        return [(a, VMEM) for a in arrays]

    (box_early,) = new_boxes("box_early", [(chips, rows, pack)])
    (box_two,) = new_boxes("box_two", [(chips, rows, pack)])
    box_near, box_one = new_boxes("box_near", [(chips, 2 * rows, pack), (chips, rows, pack)])
    box_late, box_late_two, box_end = new_boxes(
        "box_late", [(chips, n * rows, pack) for n in (2, 3, 1)]
    )
    (hats,) = new_boxes("hats", [(chips, 2 * rows, chunk)])

    def start_kernel(reads, box, kept, sent, gain, weight_in, weight_out, staged, sem, load_sems, *scratch):
        inputs, source_in, source_out, source_gain = reads
        fold, half = place()

        @pl.when(fold == STAGES[0])
        def _():
            copy = pltpu.make_async_copy(inputs.at[half, of_micro(0)], staged, sem)
            copy.start()

            @pl.when(lax.rem(lax.axis_index("dp"), 2) == 1)
            def _():
                first = load(half, (source_in, source_out), (weight_in, weight_out), load_sems)
                wait_all(first[0] + first[1])

            ready = load(half, (source_in, source_out), (weight_in, weight_out), load_sems)
            gain[...] = source_gain[pl.ds(half, 1), :]
            copy.wait()
            out = Keeper(0, scratch, box, layer=0, kept=kept)
            sent[...] = forward(staged[...], gain, weight_in, weight_out, out, ready)
            out.wait()

    class Keeper:
        def __init__(self, m, scratch, box, slot=0, layer=0, hats=None, kept=None):
            self.rows, self.kept, sems = scratch
            own = pl.ds(layer * rows + m * micro, micro)
            at = pl.ds(slot * rows + m * micro, micro)
            pairs = [(self.rows, box.at[:, at, :])]
            if hats is not None:
                pairs.append((self.rows.at[:, :, pl.ds(0, chunk)], hats.at[:, own, :]))
            if kept is not None:
                pairs.append((self.kept, kept.at[own, :]))
            self.copies = [
                pltpu.make_async_copy(source, target, sems.at[i])
                for i, (source, target) in enumerate(pairs)
            ]

        def start(self):
            for copy in self.copies:
                copy.start()

        def wait(self):
            wait_all(self.copies)

    kept_shape = pltpu.HBM((2 * rows, branch + 128), f32)
    kept_block = pltpu.VMEM((micro, branch + 128), f32)
    (kept,) = pl.pallas_call(
        lambda *refs: None, out_shape=(kept_shape,), out_specs=(HBM,), name="kept"
    )()

    copies = 3

    def keeping(n=1):
        return [
            pltpu.VMEM((n, chips, micro, pack), bf16),
            pltpu.VMEM((n, micro, branch + 128), f32),
            dma((n, copies)),
        ]

    keeping_one = [packed, kept_block, dma((copies,))]
    moved = [None] * MICROS
    box_early, kept, sent, *weights_1 = call(
        start_kernel,
        "forward_0_0",
        [(inputs, HBM), (w_in, HBM), (w_out, HBM), (gain, VMEM)],
        places=(box_early, kept),
        new=(block, row_shape, in_shape, out_shape),
        scratch=[block, dma(()), load_sems] + keeping_one,
    )
    moved[0] = send_on(sent, 0)
    for m in range(1, MICROS):

        def input_kernel(reads, box, kept, sent, staged, sem, *scratch, m=m):
            inputs, *weights = reads
            fold, half = place()

            @pl.when(fold == STAGES[0])
            def _():
                copy = pltpu.make_async_copy(inputs.at[half, of_micro(m)], staged, sem)
                copy.start()
                copy.wait()
                out = Keeper(m, scratch, box, layer=0, kept=kept)
                sent[...] = forward(staged[...], *weights, out)
                out.wait()

        box_early, kept, sent = call(
            input_kernel,
            "forward_0_%d" % m,
            [(inputs, HBM)] + in_vmem(*weights_1),
            places=(box_early, kept),
            new=(block,),
            scratch=[block, dma(())] + keeping_one,
        )
        moved[m] = send_on(sent, 0)

    def turn(weight_in, weight_out, weight_in_t, weight_out_t):
        @pl.loop(0, width // branch)
        def _(tile):
            part = pl.ds(pl.multiple_of(tile * branch, branch), branch)
            weight_in_t[:, part] = weight_in[part, :].T
            weight_out_t[part, :] = weight_out[:, part].T

    def fresh_weights(name, here, layers, plain, turned):
        def kernel(reads, *refs):
            source_in, source_out, source_gain = reads
            fold, half = place()
            sems, raw = refs[-1], refs[-3:-1]

            @pl.when(here(fold))
            def _():
                waits, at = [], 0
                for i, layer in enumerate(layers):
                    copy = half if layer == 0 else 1 - half
                    gain, *targets = refs[at : at + 1 + 2 * (plain + turned)]
                    at += 1 + 2 * (plain + turned)
                    gain[...] = source_gain[pl.ds(copy, 1), :]
                    loaded = targets[:2] if plain else raw
                    waits.append(load(copy, (source_in, source_out), loaded, sems.at[i]))
                    if turned:
                        wait_all(waits[i][0] + waits[i][1])
                        turn(*loaded, *targets[-2:])
                if not turned:
                    for wait in waits:
                        wait_all(wait[0] + wait[1])

        shapes = (row_shape,) + (in_shape, out_shape) * plain + (in_turned, out_turned) * turned
        outs = call(
            kernel,
            name,
            [(in_hbm(raw_in), HBM), (in_hbm(raw_out), HBM), (gain, VMEM)],
            new=shapes * len(layers),
            scratch=[in_shape, out_shape, dma((len(layers), 2 * LOADS))],
        )
        return [outs[i * len(shapes) : (i + 1) * len(shapes)] for i in range(len(layers))]

    def forward_kernel(stage, slots, m, reads, *refs):
        moved = reads[0]
        boxes, (hats, kept, sent, stash, stash_kept, sems) = refs[:-6], refs[-6:]
        layers = list(slots)
        weights = [reads[1 + 3 * i : 4 + 3 * i] for i in range(len(layers))]
        fold, _ = place()

        @pl.when(fold == STAGES[stage])
        def _():
            outs = [
                Keeper(
                    m,
                    (stash.at[i], stash_kept.at[i], sems.at[i]),
                    boxes[min(i, len(boxes) - 1)],
                    slot=slots[layer],
                    layer=layer,
                    hats=hats,
                    kept=kept,
                )
                for i, layer in enumerate(layers)
            ]
            for i, out in enumerate(outs):
                source = moved if i == 0 else sent
                sent[...] = forward(source[...], *weights[i], out)
            for out in outs:
                out.wait()

    def forward_stage(stage, slots, boxes, weights):
        nonlocal hats, kept
        for m in range(MICROS):
            *boxes, hats, kept, sent = call(
                functools.partial(forward_kernel, stage, slots, m),
                "forward_%d_%d" % (stage, m),
                in_vmem(moved[m], *[a for layer in slots for a in weights[layer]]),
                places=(*boxes, hats, kept),
                new=(block,),
                scratch=keeping(len(slots)),
            )
            moved[m] = send_on(sent, stage)
        return boxes

    weights = fresh_weights("load_1", lambda fold: fold == 1, (0,), 1, 0)
    (box_early,) = forward_stage(1, {0: 0}, [box_early], weights)

    def none(name, array):
        return new_boxes(name, [array.shape])[0]

    box_early, kept = lax.optimization_barrier((box_early, kept))
    got_early = lax.cond(fold_here <= 1, exchange, functools.partial(none, "none_early"), box_early)
    got_early, box_two, kept, hats, raw_in, raw_out = lax.optimization_barrier(
        (got_early, box_two, kept, hats, raw_in, raw_out)
    )
    weights = fresh_weights("load_2", lambda fold: fold == 2, (0,), 1, 0)
    (box_two,) = forward_stage(2, {0: 0}, [box_two], weights)
    raw_in, raw_out, kept = lax.optimization_barrier((raw_in, raw_out, kept))
    weights = fresh_weights("load_3", lambda fold: fold == 3, (0, 1), 1, 0)
    box_two, box_late_two = forward_stage(3, {0: 0, 1: 2}, [box_two, box_late_two], weights)
    raw_in, raw_out, kept = lax.optimization_barrier((raw_in, raw_out, kept))
    weights = fresh_weights("load_4", lambda fold: fold == 2, (1,), 1, 0)
    (box_late_two,) = forward_stage(4, {1: 2}, [box_late_two], [None, *weights])

    box_two, kept = lax.optimization_barrier((box_two, kept))
    got_two = lax.cond(fold_here >= 2, exchange, functools.partial(none, "none_two"), box_two)
    got_two, box_near, box_one, kept, hats, raw_in, raw_out = lax.optimization_barrier(
        (got_two, box_near, box_one, kept, hats, raw_in, raw_out)
    )
    (near,) = fresh_weights("load_near", lambda fold: fold <= 1, (1,), 1, 1)
    (box_one,) = forward_stage(5, {1: 0}, [box_one], [None, near[:3]])

    def middle_kernel(m, reads, box, kept, sent, staged, sem, stash, stash_kept, sems):
        moved, cotangent, gain, weight_in, weight_in_t, weight_out_t = reads
        fold, half = place()

        @pl.when(fold == STAGES[6])
        def _():
            copy = pltpu.make_async_copy(cotangent.at[half, of_micro(m)], staged, sem)
            copy.start()
            outs = [
                Keeper(m, (stash.at[i], stash_kept.at[0], sems.at[i]), box, slot=i)
                for i in range(2)
            ]
            forward(moved[...], gain, weight_in, None, outs[0])
            copy.wait()
            sent[...] = backward(
                staged[...], gain, weight_in_t, weight_out_t, outs[1], lambda: stash_kept.at[0],
                lambda chip: stash[0, chip, :, :chunk],
            )
            for out in outs:
                out.wait()

    for m in range(MICROS):
        box_near, kept, sent = call(
            functools.partial(middle_kernel, m),
            "middle_%d" % m,
            [(moved[m], VMEM), (cotangent, HBM)] + in_vmem(near[0], near[1], near[3], near[4]),
            places=(box_near, kept),
            new=(block,),
            scratch=[block, dma(())] + keeping(2),
        )
        moved[m] = send_on(sent, 6)

    def saved_rows(name, here, layer):
        def kernel(reads, hats_out, kept_out, sems):
            fold, _ = place()
            at = pl.ds(layer * rows, rows)

            @pl.when(here(fold))
            def _():
                copies = [
                    pltpu.make_async_copy(reads[0].at[chip, at, :], hats_out.at[chip], sems.at[chip])
                    for chip in range(chips)
                ]
                copies.append(pltpu.make_async_copy(reads[1].at[at, :], kept_out, sems.at[chips]))
                for copy in copies:
                    copy.start()
                wait_all(copies)

        return call(
            kernel,
            name,
            [(in_hbm(hats), HBM), (in_hbm(kept), HBM)],
            new=(pltpu.VMEM((chips, rows, chunk), bf16), pltpu.VMEM((rows, branch + 128), f32)),
            scratch=[dma((chips + 1,))],
        )

    def backward_kernel(stage, slots, m, reads, box, kept, *refs):
        moved = reads[0]
        layers = list(slots)
        weights = [reads[1 + 5 * i : 4 + 5 * i] for i in range(len(layers))]
        saved = [reads[4 + 5 * i : 6 + 5 * i] for i in range(len(layers))]
        sent = refs[0] if stage < LAST else None
        stash, stash_kept, sems = refs[-3:]
        fold, _ = place()

        @pl.when(fold == STAGES[stage])
        def _():
            outs = [
                Keeper(m, (stash.at[i], stash_kept.at[i], sems.at[i]), box, slot=slots[layer])
                for i, layer in enumerate(layers)
            ]
            for i, out in enumerate(outs):
                source = moved if i == 0 else sent
                have_hats, have = saved[i]
                result = backward(
                    source[...], *weights[i], out, lambda have=have: have.at[of_micro(m)],
                    (lambda chip, hats=have_hats: hats[chip, of_micro(m), :])
                    if sent is not None
                    else None,
                )
                if sent is not None:
                    sent[...] = result
            for out in outs:
                out.wait()

    def backward_stage(stage, slots, box, weights):
        nonlocal kept
        n = len(slots)
        for m in range(MICROS):
            box, kept, *sent = call(
                functools.partial(backward_kernel, stage, slots, m),
                "backward_%d_%d" % (stage, m),
                in_vmem(moved[m], *[a for layer in slots for a in weights[layer]]) ,
                places=(box, kept),
                new=(block,) if stage < LAST else (),
                scratch=keeping(n),
            )
            if sent:
                moved[m] = send_on(sent[0], stage)
        return box

    saved_2 = saved_rows("saved_near_2", lambda fold: fold == 1, 1)
    box_late = backward_stage(7, {1: 0}, box_late, [None, (near[0], *near[3:], *saved_2)])

    box_near, box_one, kept = lax.optimization_barrier((box_near, box_one, kept))
    got_near, got_one = lax.switch(
        jnp.minimum(fold_here, 2),
        (
            lambda near, one: (exchange(near), none("none_one", one)),
            lambda near, one: (none("none_near", near), exchange(one)),
            lambda near, one: (none("none_near", near), none("none_one", one)),
        ),
        box_near,
        box_one,
    )
    got_near, got_one, box_late, box_late_two, box_end, kept, raw_in, raw_out = lax.optimization_barrier(
        (got_near, got_one, box_late, box_late_two, box_end, kept, raw_in, raw_out)
    )
    (far_2,) = fresh_weights("turn_far_2", lambda fold: fold >= 2, (1,), 0, 1)
    far_2 = (*far_2, *saved_rows("saved_far_2", lambda fold: fold >= 2, 1))
    box_late_two = backward_stage(8, {1: 0}, box_late_two, [None, far_2])
    kept, raw_in, raw_out = lax.optimization_barrier((kept, raw_in, raw_out))
    (far_1,) = fresh_weights("turn_9", lambda fold: fold == 3, (0,), 0, 1)
    far_1 = (*far_1, *saved_rows("saved_9", lambda fold: fold == 3, 0))
    box_late_two = backward_stage(9, {1: 0, 0: 1}, box_late_two, [far_1, far_2])
    kept, raw_in, raw_out = lax.optimization_barrier((kept, raw_in, raw_out))
    (far_1,) = fresh_weights("turn_10", lambda fold: fold == 2, (0,), 0, 1)
    far_1 = (*far_1, *saved_rows("saved_10", lambda fold: fold == 2, 0))
    box_late_two = backward_stage(10, {0: 1}, box_late_two, [far_1])

    box_late_two, kept = lax.optimization_barrier((box_late_two, kept))
    got_late_two = lax.cond(
        fold_here >= 2,
        functools.partial(exchange, raw=True),
        functools.partial(none, "none_late_two"),
        box_late_two,
    )
    got_late_two, box_late, kept, hats, raw_in, raw_out = lax.optimization_barrier(
        (got_late_two, box_late, kept, hats, raw_in, raw_out)
    )
    (near_1,) = fresh_weights("turn_11", lambda fold: fold == 1, (0,), 0, 1)
    near_1 = (*near_1, *saved_rows("saved_11", lambda fold: fold == 1, 0))
    box_late = backward_stage(11, {0: 1}, box_late, [near_1])

    box_late, kept = lax.optimization_barrier((box_late, kept))
    got_late = lax.cond(
        fold_here == 1,
        functools.partial(exchange, raw=True),
        functools.partial(none, "none_late"),
        box_late,
    )
    got_late, box_end, kept, raw_in, raw_out = lax.optimization_barrier(
        (got_late, box_end, kept, raw_in, raw_out)
    )
    (near_1,) = fresh_weights("turn_12", lambda fold: fold == 0, (0,), 0, 1)
    near_1 = (*near_1, *saved_rows("saved_12", lambda fold: fold == 0, 0))
    box_end = backward_stage(LAST, {0: 0}, box_end, [near_1])

    def products(pick, reads, keep, send, whole_in, whole_out):
        _, half = place()
        core = lax.rem(lax.axis_index("dp"), 2)
        mine = pl.ds(pl.multiple_of(core * branch, branch), branch)
        theirs = pl.ds(pl.multiple_of((1 - core) * branch, branch), branch)
        narrow, wide = slice(chunk, pack), slice(0, chunk)

        def part(which, columns):
            box, slot = which
            return reads[box][:, slot * rows : (slot + 1) * rows, columns].reshape(chips * rows, -1)

        for layer, slot in ((0, half), (1, 1 - half)):
            hat, up = pick[layer]
            whole_in[...] = transposed_matmul(part(hat, wide), part(up, narrow))
            whole_out[...] = transposed_matmul(part(hat, narrow), part(up, wide))
            keep[slot, 0] = whole_in[mine, :]
            keep[slot, 1] = whole_out[:, mine]
            send[slot, 0] = whole_in[theirs, :].astype(bf16)
            send[slot, 1] = whole_out[:, theirs].astype(bf16)

    def finish(name, pick, *boxes):
        return call(
            functools.partial(products, pick),
            name,
            in_vmem(*boxes),
            new=(pltpu.VMEM((2, 2, branch, branch), f32), pltpu.VMEM((2, 2, branch, branch), bf16)),
            scratch=[pltpu.VMEM((2 * branch, branch), f32), pltpu.VMEM((branch, 2 * branch), f32)],
        )

    near_pick = (((0, 0), (1, 1)), ((2, 0), (1, 0)))
    far_pick = (((0, 0), (1, 1)), ((1, 2), (1, 0)))
    keep, send = lax.switch(
        jnp.minimum(fold_here, 2),
        (
            lambda end, late, late_two, early, near, one, two: finish(
                "products_0", (((0, 0), (1, 0)), ((2, 0), (2, 1))), early, exchange(end, raw=True), near
            ),
            lambda end, late, late_two, early, near, one, two: finish(
                "products_1", near_pick, early, late, one
            ),
            lambda end, late, late_two, early, near, one, two: finish(
                "products_2", far_pick, two, late_two
            ),
        ),
        box_end,
        got_late,
        got_late_two,
        got_early,
        got_near,
        got_one,
        got_two,
    )
    total = keep + lax.ppermute(send, "dp", [(i, i ^ 1) for i in range(parts)]).astype(f32)
    mirror = [(s, sections - 1 - s) for s in range(sections)]
    total = total[0] + lax.ppermute(total[1].astype(bf16), "section", mirror).astype(f32)
    start = lax.axis_index("dp") * branch
    own_gain = lax.dynamic_slice_in_dim(gain[0], start, branch, 0)
    own_in = lax.dynamic_slice_in_dim(raw_in[0], start, branch, 0).astype(f32)
    grad_in = total[0] * own_gain[:, None]
    grad_gain = jnp.sum(total[0] * own_in, axis=1)
    return (grad_in[None], total[1][None], grad_gain[None])


def solution(mesh):
    return jax.shard_map(
        on_device,
        mesh=mesh,
        in_specs=(
            P(None, "dp", None),
            P(None, "dp", None),
            P("section", None, None),
            P("section", None, None),
            P("section", None),
        ),
        out_specs=(P("section", "dp", None), P("section", None, "dp"), P("section", "dp")),
        check_vma=False,
    )
```

```python
import functools

import jax
import jax.numpy as jnp
from jax import lax
from jax.experimental import pallas as pl
from jax.experimental.pallas import tpu as pltpu
from jax.sharding import PartitionSpec as P

epsilon = 1e-05
STAGES = (0, 1, 2, 3, 2, 1, 0, 1, 2, 3, 2, 1, 0)
LAST = len(STAGES) - 1
MICROS = 2
bf16 = jnp.bfloat16
f32 = jnp.float32
VMEM = pl.BlockSpec(memory_space=pltpu.VMEM)
HBM = pl.BlockSpec(memory_space=pltpu.HBM)
LOADS = 8
MIB = 2**20


def matmul(left, right):
    return jnp.dot(left, right, preferred_element_type=f32)


def transposed_matmul(left, right):
    return lax.dot_general(left, right, (((0,), (0,)), ((), ())), preferred_element_type=f32)


def place():
    sections = lax.axis_size("section")
    position = lax.axis_index("section")
    half = (position >= sections // 2).astype(jnp.int32)
    fold = jnp.where(half == 0, position, sections - 1 - position)
    return fold, half


def call(body, name, reads, updates=(), places=(), new=(), scratch=(), limit=16):
    n_read, n_update, n_place = len(reads), len(updates), len(places)

    def kernel(*refs):
        ins, outs = refs[: n_read + n_update + n_place], refs[n_read + n_update + n_place :]
        for old, now in zip(ins[n_read : n_read + n_update], outs):
            now[...] = old[...]
        body(ins[:n_read], *outs)

    shapes = [pltpu.VMEM(a.shape, a.dtype) for a in updates]
    shapes += [pltpu.HBM(a.shape, a.dtype) for a in places]
    shapes += list(new)
    kept = [VMEM] * n_update + [HBM] * n_place
    return pl.pallas_call(
        kernel,
        out_shape=tuple(shapes),
        in_specs=[spec for _, spec in reads] + kept,
        out_specs=tuple(kept + [VMEM] * len(new)),
        input_output_aliases={n_read + i: i for i in range(n_update + n_place)},
        scratch_shapes=list(scratch),
        compiler_params=pltpu.CompilerParams(vmem_limit_bytes=limit * MIB),
        cost_estimate=pl.CostEstimate(flops=1, bytes_accessed=1, transcendentals=0),
        name=name,
    )(*[a for a, _ in reads], *updates, *places)


def load(copy, sources, targets, sems):
    waits = []
    for which, (source, target) in enumerate(zip(sources, targets)):
        size = source.shape[1] // LOADS
        pieces = []
        for i in range(LOADS):
            part = pl.ds(i * size, size)
            pieces.append(
                pltpu.make_async_copy(
                    source.at[copy, part], target.at[part], sems.at[which * LOADS + i]
                )
            )
        for piece in pieces:
            piece.start()
        waits.append(pieces)
    return waits


def wait_all(pieces):
    for piece in pieces:
        piece.wait()


def forward(source, gain, weight_in, weight_out, out, ready=None):
    chips = out.rows.shape[0]
    micro, width = source.shape
    branch = weight_in.shape[1]
    chunk = width // chips
    wide = source.astype(f32)
    scaling = lax.rsqrt(jnp.mean(wide * wide, axis=-1, keepdims=True) + epsilon)
    normal = wide * scaling
    if ready is not None:
        wait_all(ready[0])
    before = matmul((normal * gain[...]).astype(bf16), weight_in[...])
    inner = (before * jax.nn.sigmoid(before)).astype(bf16)
    out.kept[:, :branch] = before
    out.kept[:, branch:] = jnp.broadcast_to(scaling, (micro, 128))
    for chip in range(chips):
        out.rows[chip, :, :chunk] = normal[:, chip * chunk : (chip + 1) * chunk].astype(bf16)
        out.rows[chip, :, chunk:] = inner
    out.start()
    if ready is not None:
        wait_all(ready[1])
    if weight_out is not None:
        return (wide + matmul(inner, weight_out[...])).astype(bf16)


def backward(grad, gain, weight_in_t, weight_out_t, out, saved, hats):
    chips = out.rows.shape[0]
    width = grad.shape[1]
    branch = weight_in_t.shape[0]
    chunk = width // chips
    d_inner = matmul(grad, weight_out_t[...])
    kept = saved()
    before = kept[:, :branch]
    sigma = jax.nn.sigmoid(before)
    delta = (d_inner * sigma * (1.0 + before * (1.0 - sigma))).astype(bf16)
    for chip in range(chips):
        out.rows[chip, :, :chunk] = grad[:, chip * chunk : (chip + 1) * chunk]
        out.rows[chip, :, chunk:] = delta
    out.start()
    if hats is None:
        return None
    mixed = jnp.sum(delta.astype(f32) * before, axis=-1, keepdims=True) / width
    scaled = matmul(delta, weight_in_t[...]) * gain[...]
    scaling = kept[:, branch : branch + 1]
    result = []
    for chip in range(chips):
        part = slice(chip * chunk, (chip + 1) * chunk)
        normal = hats(chip).astype(f32)
        result.append(
            (grad[:, part].astype(f32) + scaling * (scaled[:, part] - normal * mixed)).astype(bf16)
        )
    return jnp.concatenate(result, axis=1)


def on_device(inputs, cotangent, w_in, w_out, gain):
    sections = lax.axis_size("section")
    parts = lax.axis_size("dp")
    chips = parts // 2
    rows, width = inputs.shape[1:]
    micro = rows // MICROS
    branch = w_in.shape[2]
    chunk = width // chips
    pack = chunk + branch

    def in_hbm(array):
        return pltpu.with_memory_space_constraint(array, pltpu.HBM)

    raw_in, raw_out = w_in, w_out
    inputs, cotangent, w_in, w_out = map(in_hbm, (inputs, cotangent, w_in, w_out))
    dma = pltpu.SemaphoreType.DMA
    block = pltpu.VMEM((micro, width), bf16)
    packed = pltpu.VMEM((chips, micro, pack), bf16)
    in_shape, out_shape = pltpu.VMEM((width, branch), bf16), pltpu.VMEM((branch, width), bf16)
    in_turned, out_turned = out_shape, in_shape
    row_shape = pltpu.VMEM((1, width), f32)
    load_sems = dma((2 * LOADS,))
    fold_here, _ = place()
    same_core = [list(range(core, parts, 2)) for core in range(2)]

    def of_micro(m):
        return pl.ds(m * micro, micro)

    def send_on(sent, stage):
        a, b = STAGES[stage], STAGES[stage + 1]
        pairs = [(a, b), (sections - 1 - a, sections - 1 - b)]
        return lax.ppermute(sent, "section", pairs)

    def copy_kernel(reads, target, sems):
        copies = [
            pltpu.make_async_copy(reads[0].at[chip], target.at[chip], sems.at[chip])
            for chip in range(chips)
        ]
        for copy in copies:
            copy.start()
        wait_all(copies)

    def exchange(array, raw=False):
        array = lax.all_to_all(array, "dp", 0, 0, axis_index_groups=same_core, tiled=False)
        if raw:
            return array
        array = pltpu.with_memory_space_constraint(array, pltpu.VMEM)
        (target,) = new_boxes("unstage_box", [array.shape])
        (target,) = call(copy_kernel, "unstage", [(array, VMEM)], places=(target,), scratch=[dma((chips,))])
        return target

    def new_boxes(name, shapes):
        shapes = [pltpu.HBM(shape, bf16) for shape in shapes]
        return pl.pallas_call(
            lambda *refs: None, out_shape=tuple(shapes), out_specs=(HBM,) * len(shapes), name=name
        )()

    def in_vmem(*arrays):
        return [(a, VMEM) for a in arrays]

    (box_early,) = new_boxes("box_early", [(chips, rows, pack)])
    (box_two,) = new_boxes("box_two", [(chips, rows, pack)])
    box_near, box_one = new_boxes("box_near", [(chips, 2 * rows, pack), (chips, rows, pack)])
    box_late, box_late_two, box_end = new_boxes(
        "box_late", [(chips, n * rows, pack) for n in (2, 3, 1)]
    )
    (hats,) = new_boxes("hats", [(chips, 2 * rows, chunk)])

    def start_kernel(reads, box, kept, sent, gain, weight_in, weight_out, staged, sem, load_sems, *scratch):
        inputs, source_in, source_out, source_gain = reads
        fold, half = place()

        @pl.when(fold == STAGES[0])
        def _():
            copy = pltpu.make_async_copy(inputs.at[half, of_micro(0)], staged, sem)
            copy.start()
            ready = load(half, (source_in, source_out), (weight_in, weight_out), load_sems)
            gain[...] = source_gain[pl.ds(half, 1), :]
            copy.wait()
            out = Keeper(0, scratch, box, layer=0, kept=kept)
            sent[...] = forward(staged[...], gain, weight_in, weight_out, out, ready)
            out.wait()

    class Keeper:
        def __init__(self, m, scratch, box, slot=0, layer=0, hats=None, kept=None):
            self.rows, self.kept, sems = scratch
            own = pl.ds(layer * rows + m * micro, micro)
            at = pl.ds(slot * rows + m * micro, micro)
            pairs = [(self.rows, box.at[:, at, :])]
            if hats is not None:
                pairs.append((self.rows.at[:, :, pl.ds(0, chunk)], hats.at[:, own, :]))
            if kept is not None:
                pairs.append((self.kept, kept.at[own, :]))
            self.copies = [
                pltpu.make_async_copy(source, target, sems.at[i])
                for i, (source, target) in enumerate(pairs)
            ]

        def start(self):
            for copy in self.copies:
                copy.start()

        def wait(self):
            wait_all(self.copies)

    kept_shape = pltpu.HBM((2 * rows, branch + 128), f32)
    kept_block = pltpu.VMEM((micro, branch + 128), f32)
    (kept,) = pl.pallas_call(
        lambda *refs: None, out_shape=(kept_shape,), out_specs=(HBM,), name="kept"
    )()

    copies = 3

    def keeping(n=1):
        return [
            pltpu.VMEM((n, chips, micro, pack), bf16),
            pltpu.VMEM((n, micro, branch + 128), f32),
            dma((n, copies)),
        ]

    keeping_one = [packed, kept_block, dma((copies,))]
    moved = [None] * MICROS
    box_early, kept, sent, *weights_1 = call(
        start_kernel,
        "forward_0_0",
        [(inputs, HBM), (w_in, HBM), (w_out, HBM), (gain, VMEM)],
        places=(box_early, kept),
        new=(block, row_shape, in_shape, out_shape),
        scratch=[block, dma(()), load_sems] + keeping_one,
    )
    moved[0] = send_on(sent, 0)
    for m in range(1, MICROS):

        def input_kernel(reads, box, kept, sent, staged, sem, *scratch, m=m):
            inputs, *weights = reads
            fold, half = place()

            @pl.when(fold == STAGES[0])
            def _():
                copy = pltpu.make_async_copy(inputs.at[half, of_micro(m)], staged, sem)
                copy.start()
                copy.wait()
                out = Keeper(m, scratch, box, layer=0, kept=kept)
                sent[...] = forward(staged[...], *weights, out)
                out.wait()

        box_early, kept, sent = call(
            input_kernel,
            "forward_0_%d" % m,
            [(inputs, HBM)] + in_vmem(*weights_1),
            places=(box_early, kept),
            new=(block,),
            scratch=[block, dma(())] + keeping_one,
        )
        moved[m] = send_on(sent, 0)

    def turn(weight_in, weight_out, weight_in_t, weight_out_t):
        @pl.loop(0, width // branch)
        def _(tile):
            part = pl.ds(pl.multiple_of(tile * branch, branch), branch)
            weight_in_t[:, part] = weight_in[part, :].T
            weight_out_t[part, :] = weight_out[:, part].T

    def fresh_weights(name, here, layers, plain, turned):
        def kernel(reads, *refs):
            source_in, source_out, source_gain = reads
            fold, half = place()
            sems, raw = refs[-1], refs[-3:-1]

            @pl.when(here(fold))
            def _():
                waits, at = [], 0
                for i, layer in enumerate(layers):
                    copy = half if layer == 0 else 1 - half
                    gain, *targets = refs[at : at + 1 + 2 * (plain + turned)]
                    at += 1 + 2 * (plain + turned)
                    gain[...] = source_gain[pl.ds(copy, 1), :]
                    loaded = targets[:2] if plain else raw
                    waits.append(load(copy, (source_in, source_out), loaded, sems.at[i]))
                    if turned:
                        wait_all(waits[i][0] + waits[i][1])
                        turn(*loaded, *targets[-2:])
                if not turned:
                    for wait in waits:
                        wait_all(wait[0] + wait[1])

        shapes = (row_shape,) + (in_shape, out_shape) * plain + (in_turned, out_turned) * turned
        outs = call(
            kernel,
            name,
            [(in_hbm(raw_in), HBM), (in_hbm(raw_out), HBM), (gain, VMEM)],
            new=shapes * len(layers),
            scratch=[in_shape, out_shape, dma((len(layers), 2 * LOADS))],
        )
        return [outs[i * len(shapes) : (i + 1) * len(shapes)] for i in range(len(layers))]

    def forward_kernel(stage, slots, m, reads, *refs):
        moved = reads[0]
        boxes, (hats, kept, sent, stash, stash_kept, sems) = refs[:-6], refs[-6:]
        layers = list(slots)
        weights = [reads[1 + 3 * i : 4 + 3 * i] for i in range(len(layers))]
        fold, _ = place()

        @pl.when(fold == STAGES[stage])
        def _():
            outs = [
                Keeper(
                    m,
                    (stash.at[i], stash_kept.at[i], sems.at[i]),
                    boxes[min(i, len(boxes) - 1)],
                    slot=slots[layer],
                    layer=layer,
                    hats=hats,
                    kept=kept,
                )
                for i, layer in enumerate(layers)
            ]
            for i, out in enumerate(outs):
                source = moved if i == 0 else sent
                sent[...] = forward(source[...], *weights[i], out)
            for out in outs:
                out.wait()

    def forward_stage(stage, slots, boxes, weights):
        nonlocal hats, kept
        for m in range(MICROS):
            *boxes, hats, kept, sent = call(
                functools.partial(forward_kernel, stage, slots, m),
                "forward_%d_%d" % (stage, m),
                in_vmem(moved[m], *[a for layer in slots for a in weights[layer]]),
                places=(*boxes, hats, kept),
                new=(block,),
                scratch=keeping(len(slots)),
            )
            moved[m] = send_on(sent, stage)
        return boxes

    weights = fresh_weights("load_1", lambda fold: fold == 1, (0,), 1, 0)
    (box_early,) = forward_stage(1, {0: 0}, [box_early], weights)

    def none(name, array):
        return new_boxes(name, [array.shape])[0]

    box_early, kept = lax.optimization_barrier((box_early, kept))
    got_early = lax.cond(fold_here <= 1, exchange, functools.partial(none, "none_early"), box_early)
    got_early, box_two, kept, hats, raw_in, raw_out = lax.optimization_barrier(
        (got_early, box_two, kept, hats, raw_in, raw_out)
    )
    weights = fresh_weights("load_2", lambda fold: fold == 2, (0,), 1, 0)
    (box_two,) = forward_stage(2, {0: 0}, [box_two], weights)
    raw_in, raw_out, kept = lax.optimization_barrier((raw_in, raw_out, kept))
    weights = fresh_weights("load_3", lambda fold: fold == 3, (0, 1), 1, 0)
    box_two, box_late_two = forward_stage(3, {0: 0, 1: 2}, [box_two, box_late_two], weights)
    raw_in, raw_out, kept = lax.optimization_barrier((raw_in, raw_out, kept))
    weights = fresh_weights("load_4", lambda fold: fold == 2, (1,), 1, 0)
    (box_late_two,) = forward_stage(4, {1: 2}, [box_late_two], [None, *weights])

    box_two, kept = lax.optimization_barrier((box_two, kept))
    got_two = lax.cond(fold_here >= 2, exchange, functools.partial(none, "none_two"), box_two)
    got_two, box_near, box_one, kept, hats, raw_in, raw_out = lax.optimization_barrier(
        (got_two, box_near, box_one, kept, hats, raw_in, raw_out)
    )
    (near,) = fresh_weights("load_near", lambda fold: fold <= 1, (1,), 1, 1)
    (box_one,) = forward_stage(5, {1: 0}, [box_one], [None, near[:3]])

    def middle_kernel(m, reads, box, kept, sent, staged, sem, stash, stash_kept, sems):
        moved, cotangent, gain, weight_in, weight_in_t, weight_out_t = reads
        fold, half = place()

        @pl.when(fold == STAGES[6])
        def _():
            copy = pltpu.make_async_copy(cotangent.at[half, of_micro(m)], staged, sem)
            copy.start()
            outs = [
                Keeper(m, (stash.at[i], stash_kept.at[0], sems.at[i]), box, slot=i)
                for i in range(2)
            ]
            forward(moved[...], gain, weight_in, None, outs[0])
            copy.wait()
            sent[...] = backward(
                staged[...], gain, weight_in_t, weight_out_t, outs[1], lambda: stash_kept.at[0],
                lambda chip: stash[0, chip, :, :chunk],
            )
            for out in outs:
                out.wait()

    for m in range(MICROS):
        box_near, kept, sent = call(
            functools.partial(middle_kernel, m),
            "middle_%d" % m,
            [(moved[m], VMEM), (cotangent, HBM)] + in_vmem(near[0], near[1], near[3], near[4]),
            places=(box_near, kept),
            new=(block,),
            scratch=[block, dma(())] + keeping(2),
        )
        moved[m] = send_on(sent, 6)

    def saved_rows(name, here, layer):
        def kernel(reads, hats_out, kept_out, sems):
            fold, _ = place()
            at = pl.ds(layer * rows, rows)

            @pl.when(here(fold))
            def _():
                copies = [
                    pltpu.make_async_copy(reads[0].at[chip, at, :], hats_out.at[chip], sems.at[chip])
                    for chip in range(chips)
                ]
                copies.append(pltpu.make_async_copy(reads[1].at[at, :], kept_out, sems.at[chips]))
                for copy in copies:
                    copy.start()
                wait_all(copies)

        return call(
            kernel,
            name,
            [(in_hbm(hats), HBM), (in_hbm(kept), HBM)],
            new=(pltpu.VMEM((chips, rows, chunk), bf16), pltpu.VMEM((rows, branch + 128), f32)),
            scratch=[dma((chips + 1,))],
        )

    def backward_kernel(stage, slots, m, reads, box, kept, *refs):
        moved = reads[0]
        layers = list(slots)
        weights = [reads[1 + 5 * i : 4 + 5 * i] for i in range(len(layers))]
        saved = [reads[4 + 5 * i : 6 + 5 * i] for i in range(len(layers))]
        sent = refs[0] if stage < LAST else None
        stash, stash_kept, sems = refs[-3:]
        fold, _ = place()

        @pl.when(fold == STAGES[stage])
        def _():
            outs = [
                Keeper(m, (stash.at[i], stash_kept.at[i], sems.at[i]), box, slot=slots[layer])
                for i, layer in enumerate(layers)
            ]
            for i, out in enumerate(outs):
                source = moved if i == 0 else sent
                have_hats, have = saved[i]
                result = backward(
                    source[...], *weights[i], out, lambda have=have: have.at[of_micro(m)],
                    (lambda chip, hats=have_hats: hats[chip, of_micro(m), :])
                    if sent is not None
                    else None,
                )
                if sent is not None:
                    sent[...] = result
            for out in outs:
                out.wait()

    def backward_stage(stage, slots, box, weights):
        nonlocal kept
        n = len(slots)
        for m in range(MICROS):
            box, kept, *sent = call(
                functools.partial(backward_kernel, stage, slots, m),
                "backward_%d_%d" % (stage, m),
                in_vmem(moved[m], *[a for layer in slots for a in weights[layer]]) ,
                places=(box, kept),
                new=(block,) if stage < LAST else (),
                scratch=keeping(n),
            )
            if sent:
                moved[m] = send_on(sent[0], stage)
        return box

    saved_2 = saved_rows("saved_near_2", lambda fold: fold == 1, 1)
    box_late = backward_stage(7, {1: 0}, box_late, [None, (near[0], *near[3:], *saved_2)])

    box_near, box_one, kept = lax.optimization_barrier((box_near, box_one, kept))
    got_near, got_one = lax.switch(
        jnp.minimum(fold_here, 2),
        (
            lambda near, one: (exchange(near), none("none_one", one)),
            lambda near, one: (none("none_near", near), exchange(one)),
            lambda near, one: (none("none_near", near), none("none_one", one)),
        ),
        box_near,
        box_one,
    )
    got_near, got_one, box_late, box_late_two, box_end, kept, raw_in, raw_out = lax.optimization_barrier(
        (got_near, got_one, box_late, box_late_two, box_end, kept, raw_in, raw_out)
    )
    (far_2,) = fresh_weights("turn_far_2", lambda fold: fold >= 2, (1,), 0, 1)
    far_2 = (*far_2, *saved_rows("saved_far_2", lambda fold: fold >= 2, 1))
    box_late_two = backward_stage(8, {1: 0}, box_late_two, [None, far_2])
    kept, raw_in, raw_out = lax.optimization_barrier((kept, raw_in, raw_out))
    (far_1,) = fresh_weights("turn_9", lambda fold: fold == 3, (0,), 0, 1)
    far_1 = (*far_1, *saved_rows("saved_9", lambda fold: fold == 3, 0))
    box_late_two = backward_stage(9, {1: 0, 0: 1}, box_late_two, [far_1, far_2])
    kept, raw_in, raw_out = lax.optimization_barrier((kept, raw_in, raw_out))
    (far_1,) = fresh_weights("turn_10", lambda fold: fold == 2, (0,), 0, 1)
    far_1 = (*far_1, *saved_rows("saved_10", lambda fold: fold == 2, 0))
    box_late_two = backward_stage(10, {0: 1}, box_late_two, [far_1])

    def products(pick, reads, keep, send, whole_in, whole_out):
        _, half = place()
        core = lax.rem(lax.axis_index("dp"), 2)
        mine = pl.ds(pl.multiple_of(core * branch, branch), branch)
        theirs = pl.ds(pl.multiple_of((1 - core) * branch, branch), branch)
        narrow, wide = slice(chunk, pack), slice(0, chunk)

        def part(which, columns):
            box, slot = which
            return reads[box][:, slot * rows : (slot + 1) * rows, columns].reshape(chips * rows, -1)

        for layer, slot in ((0, half), (1, 1 - half)):
            hat, up = pick[layer]
            whole_in[...] = transposed_matmul(part(hat, wide), part(up, narrow))
            whole_out[...] = transposed_matmul(part(hat, narrow), part(up, wide))
            keep[slot, 0] = whole_in[mine, :]
            keep[slot, 1] = whole_out[:, mine]
            send[slot, 0] = whole_in[theirs, :].astype(bf16)
            send[slot, 1] = whole_out[:, theirs].astype(bf16)

    def finish(name, pick, *boxes):
        return call(
            functools.partial(products, pick),
            name,
            in_vmem(*boxes),
            new=(pltpu.VMEM((2, 2, branch, branch), f32), pltpu.VMEM((2, 2, branch, branch), bf16)),
            scratch=[pltpu.VMEM((2 * branch, branch), f32), pltpu.VMEM((branch, 2 * branch), f32)],
        )

    def nothing(*_):
        return call(
            lambda reads, keep, send: None,
            "nothing",
            [],
            new=(pltpu.VMEM((2, 2, branch, branch), f32), pltpu.VMEM((2, 2, branch, branch), bf16)),
        )

    box_late_two, kept = lax.optimization_barrier((box_late_two, kept))
    done_far = lax.cond(
        fold_here >= 2,
        lambda late, two: finish(
            "products_far", (((0, 0), (1, 1)), ((1, 2), (1, 0))), two, exchange(late, raw=True)
        ),
        nothing,
        box_late_two,
        got_two,
    )
    done_far, box_late, kept, hats, raw_in, raw_out = lax.optimization_barrier(
        (done_far, box_late, kept, hats, raw_in, raw_out)
    )
    (near_1,) = fresh_weights("turn_11", lambda fold: fold == 1, (0,), 0, 1)
    near_1 = (*near_1, *saved_rows("saved_11", lambda fold: fold == 1, 0))
    box_late = backward_stage(11, {0: 1}, box_late, [near_1])

    box_late, kept = lax.optimization_barrier((box_late, kept))
    done_one = lax.cond(
        fold_here == 1,
        lambda late, early, one: finish(
            "products_one", (((0, 0), (1, 1)), ((2, 0), (1, 0))), early, exchange(late, raw=True), one
        ),
        nothing,
        box_late,
        got_early,
        got_one,
    )
    done_one, box_end, kept, raw_in, raw_out = lax.optimization_barrier(
        (done_one, box_end, kept, raw_in, raw_out)
    )
    (near_1,) = fresh_weights("turn_12", lambda fold: fold == 0, (0,), 0, 1)
    near_1 = (*near_1, *saved_rows("saved_12", lambda fold: fold == 0, 0))
    box_end = backward_stage(LAST, {0: 0}, box_end, [near_1])

    keep, send = lax.switch(
        jnp.minimum(fold_here, 2),
        (
            lambda end, early, near, one, far: finish(
                "products_0", (((0, 0), (1, 0)), ((2, 0), (2, 1))), early, exchange(end, raw=True), near
            ),
            lambda end, early, near, one, far: one,
            lambda end, early, near, one, far: far,
        ),
        box_end,
        got_early,
        got_near,
        tuple(done_one),
        tuple(done_far),
    )
    total = keep + lax.ppermute(send, "dp", [(i, i ^ 1) for i in range(parts)]).astype(f32)
    mirror = [(s, sections - 1 - s) for s in range(sections)]
    total = total[0] + lax.ppermute(total[1].astype(bf16), "section", mirror).astype(f32)
    start = lax.axis_index("dp") * branch
    own_gain = lax.dynamic_slice_in_dim(gain[0], start, branch, 0)
    own_in = lax.dynamic_slice_in_dim(raw_in[0], start, branch, 0).astype(f32)
    grad_in = total[0] * own_gain[:, None]
    grad_gain = jnp.sum(total[0] * own_in, axis=1)
    return (grad_in[None], total[1][None], grad_gain[None])


def solution(mesh):
    return jax.shard_map(
        on_device,
        mesh=mesh,
        in_specs=(
            P(None, "dp", None),
            P(None, "dp", None),
            P("section", None, None),
            P("section", None, None),
            P("section", None),
        ),
        out_specs=(P("section", "dp", None), P("section", None, "dp"), P("section", "dp")),
        check_vma=False,
    )
```
